128 devices in a mesh: gx: 16 (over y, x), gy: 8 (over z, core).
Axes of the slice: x: 4, y: 4, z: 4, core: 2. Of those that a mesh axis runs over, the one named last changes fastest.
Arguments:
- waveforms: bfloat16 [256, 3, 1536], P(('gx', 'gy')), may hold values from -100 to 100
- templates: bfloat16 [4096, 8, 1536], P(('gx', 'gy')), may hold values from -100 to 100
- tpl_stations: int32 [4096, 8], P(('gx', 'gy')), may hold values from 0 to 255, all different within a row; in each aligned block of 32 rows (0 to 31, 32 to 63, ...) at most 2 rows name the same one
- det_station: int32 [8192], P(('gx', 'gy')), may hold values from 0 to 1
- det_time: int32 [8192], P(('gx', 'gy')), may hold values from 64 to 1216
- partner: int32 [8192, 4], P(('gx', 'gy')), may hold values from 0 to 63
Outputs:
- stack: float32 [4096, 1024], P(('gx', 'gy'))
- diffcc: float32 [8192, 4, 128], P(('gx', 'gy'))
The draws below stay inside these ranges and needn't reach their ends.
Inputs may be any that keep to these rules, and one draw needn't show every extreme that they name: `tpl_stations`: each row names 8 different stations; among the templates of one station group no station is named more than 2 times.
All inputs are finite; a program needn't handle non-finite values.
Results may differ from the reference program's by a relative error of at most 0.0007.
Values may be sent and summed in bfloat16 or wider, within the bound.
A program may use at most 128 MiB of HBM per device.

```python
import math
import jax
import jax.numpy as jnp
import numpy as np
from jax import lax

STA_DEV = 2
TPL_DEV = 32
K = 8
TLEN = 512
NLAG = 1024
DET_DEV = 64
W = 256
DTLAG = 128
STATIONS = 256
TEMPLATES = 4096
DETECTIONS = 8192
SAMPLES = 1536
CAP = 2
N_GX = 16
N_GY = 8


def draw_waveforms(key, part):
    first, second = jax.random.split(key, 2)
    shape = (STATIONS, 3, SAMPLES)
    segments = (SAMPLES + 63) // 64
    envelope = jnp.exp(jax.random.uniform(second, (STATIONS, 3, segments), jnp.float32, 0.0, math.log(10.0)))
    envelope = jnp.repeat(envelope, 64, axis=2)[:, :, :SAMPLES]
    noise = jax.random.normal(first, shape, jnp.float32)
    return jnp.clip(noise * envelope, -100.0, 100.0).astype(jnp.bfloat16)


def draw_templates(key, part):
    first, second = jax.random.split(key, 2)
    shape = (TEMPLATES, K, 3, TLEN)
    scales = jnp.exp(jax.random.uniform(second, (TEMPLATES, K, 3, 1), jnp.float32, 0.0, math.log(10.0)))
    noise = jax.random.normal(first, shape, jnp.float32)
    return jnp.clip(noise * scales, -100.0, 100.0).reshape(TEMPLATES, K, 3 * TLEN).astype(jnp.bfloat16)


def place_ends(result, key, low, largest):
    spot = [jax.random.randint(jax.random.fold_in(key, axis), (), 0, length) for axis, length in enumerate(result.shape)]
    main_axis = result.shape.index(max(result.shape))
    neighbour = spot[:main_axis] + [(spot[main_axis] + 1) % result.shape[main_axis]] + spot[main_axis + 1:]
    return result.at[tuple(spot)].set(low).at[tuple(neighbour)].set(largest)


def routed_block(own_key, own, number, rows, amount, top, bound, skew):
    sequence = jax.random.permutation(own_key, amount)
    packed, ordinary = shares(amount, rows * top, bound, skew, True), shares(amount, rows * top, bound, skew, False)
    places = jnp.arange(amount)

    def named(lengths, rotation):
        used = int((lengths > 0).sum())
        fixed = max(1, used // 4)
        moved = fixed + (places - fixed + rotation * (used - fixed)) % max(1, amount - fixed)
        return jnp.zeros((amount,), jnp.int32).at[sequence[jnp.where(places < fixed, places, moved)]].set(jnp.asarray(lengths, jnp.int32))

    lengths = jnp.where(number % 4 == 0, named(packed, number // 4), named(ordinary, number - number // 4 - 1))
    mixed = jax.random.permutation(jax.random.fold_in(own, 3), amount)
    donor, taker = mixed[0:amount // 2 * 2:2], mixed[1:amount // 2 * 2:2]
    slack = jnp.minimum(lengths[donor] - 1, bound - lengths[taker]) // 2
    slack = jnp.where((donor == sequence[0]) | (taker == sequence[0]) | (lengths[taker] == 0), 0, jnp.maximum(slack, 0))
    moved = jax.random.randint(jax.random.fold_in(own, 4), (amount // 2,), 0, 1 << 20) % (slack + 1)
    lengths = lengths.at[donor].add(-moved).at[taker].add(moved)
    items = jnp.searchsorted(jnp.cumsum(lengths), jnp.arange(rows * top), side="right").astype(jnp.int32)
    listing = items.reshape(top, rows).T
    listing = listing[jax.random.permutation(jax.random.fold_in(own, 1), rows)]
    rotation = jax.random.randint(jax.random.fold_in(own, 2), (rows, 1), 0, top)
    return jnp.take_along_axis(listing, (jnp.arange(top)[None, :] + rotation) % top, axis=1)


def shares(count, total, most, slope, full):
    weights = [(1 << 20) // math.isqrt(rank ** slope) + 1 for rank in range(1, count + 1)]
    largest = most if full else min(most, max(-(-total // count), total * weights[0] // sum(weights)))
    least = 1 if total - largest >= count - 1 else 0
    counts, rest = [largest] + [least] * (count - 1), total - largest - least * (count - 1)
    while rest > 0:
        candidates = [i for i in range(1, count) if counts[i] < largest] or [i for i in range(1, count) if counts[i] < most]
        whole, remaining = sum([weights[i] for i in candidates]), rest
        for i in candidates:
            addition = min(most - counts[i], max(1, remaining * weights[i] // whole), rest)
            counts[i] = counts[i] + addition
            rest = rest - addition
    return np.array(counts)


def setup_inputs(seed: int = 0) -> dict:
    splits = jax.random.split(jax.random.key(seed), 7)
    waveforms = draw_waveforms(jax.random.fold_in(splits[6], 71), 0)
    templates = draw_templates(jax.random.fold_in(splits[6], 71), 0)
    tpl_stations_keys = jax.random.split(jax.random.fold_in(splits[2], 1), TEMPLATES // TPL_DEV)
    tpl_stations_turns = jax.random.permutation(jax.random.fold_in(splits[2], 3), TEMPLATES // TPL_DEV)
    tpl_stations = jax.vmap(lambda own, number: routed_block(jax.random.fold_in(splits[2], 2), own, number, TPL_DEV, STATIONS, K, CAP, 2))(tpl_stations_keys, tpl_stations_turns).reshape((TEMPLATES, K))
    det_station = place_ends(jax.random.randint(splits[3], (DETECTIONS,), 0, STA_DEV), jax.random.fold_in(splits[3], 1), 0, STA_DEV - 1).astype(jnp.int32)
    det_time = place_ends(jax.random.randint(splits[4], (DETECTIONS,), DTLAG // 2, SAMPLES - W - DTLAG // 2 + 1), jax.random.fold_in(splits[4], 1), DTLAG // 2, (SAMPLES - W - DTLAG // 2 + 1) - 1).astype(jnp.int32)
    partner = place_ends(jax.random.randint(splits[5], (DETECTIONS, 4), 0, DET_DEV), jax.random.fold_in(splits[5], 1), 0, DET_DEV - 1).astype(jnp.int32)
    return {"waveforms": waveforms, "templates": templates, "tpl_stations": tpl_stations, "det_station": det_station, "det_time": det_time, "partner": partner}


def correlate_block(block, data_freq, win_mean, nfft):
    tiles, ids = block
    tiles_f = tiles.astype(jnp.float32).reshape(tiles.shape[0], K, 3, TLEN)
    tile_mean = lax.optimization_barrier(jnp.mean(tiles_f * tiles_f, axis=(2, 3)))
    tile_freq = jnp.fft.rfft(tiles_f, n=nfft, axis=-1)
    product = lax.optimization_barrier(jnp.sum(data_freq[ids] * jnp.conj(tile_freq), axis=2))
    lagged = jnp.fft.irfft(product, n=nfft, axis=-1)[:, :, :NLAG]
    scaled = lagged / jnp.sqrt(3 * TLEN * (tile_mean[:, :, None] + 1e-06) * (win_mean[ids] + 1e-06))
    return lax.optimization_barrier(jnp.sum(scaled, axis=1)) / jnp.sqrt(jnp.float32(K))

def reference(waveforms, templates, tpl_stations, det_station, det_time, partner):
    data = waveforms.astype(jnp.float32)
    nfft = 1 << (SAMPLES - 1).bit_length()
    data_freq = jnp.fft.rfft(data, n=nfft, axis=-1)
    energy = lax.optimization_barrier(jnp.sum(data * data, axis=1))
    zero = jnp.zeros((), energy.dtype)
    window_sum = lax.reduce_window(energy, zero, lax.add, (1, TLEN), (1, 1), 'VALID')
    win_mean = window_sum[:, :NLAG] / (3 * TLEN)
    groups = N_GX * N_GY
    blocks = (templates.reshape(groups, TPL_DEV, K, 3 * TLEN), tpl_stations.reshape(groups, TPL_DEV, K))
    stack = lax.map(lambda blk: correlate_block(blk, data_freq, win_mean, nfft), blocks)
    stack = stack.reshape(TEMPLATES, NLAG)
    index = jnp.arange(DETECTIONS, dtype=jnp.int32)
    group = index // DET_DEV
    column = group // N_GY
    row = group % N_GY
    station = group * STA_DEV + det_station
    half = DTLAG // 2

    def cut(sta, start, size):
        return lax.dynamic_slice(data, (sta, jnp.int32(0), start), (1, 3, size))[0]
    local = jax.vmap(lambda s, t: cut(s, t, W))(station, det_time)
    wide = jax.vmap(lambda s, t: cut(s, t - half, W + DTLAG))(station, det_time - 0)
    wsize = W + DTLAG
    nwin = 1 << (wsize - 1).bit_length()
    local_freq = jnp.fft.rfft(local, n=nwin, axis=-1)
    local_mean = lax.optimization_barrier(jnp.mean(local * local, axis=(1, 2)))
    moves = ((1, 0), (-1, 0), (0, 1), (0, -1))
    outs = []
    for direction in range(4):
        nx = column + moves[direction][0]
        ny = row + moves[direction][1]
        valid = (nx >= 0) & (nx < N_GX) & (ny >= 0) & (ny < N_GY)
        other = jnp.clip(nx, 0, N_GX - 1) * N_GY + jnp.clip(ny, 0, N_GY - 1)
        target = other * DET_DEV + partner[:, direction]
        piece = wide[target] * valid.astype(jnp.float32)[:, None, None]
        piece_freq = jnp.fft.rfft(piece, n=nwin, axis=-1)
        lagged = jnp.fft.irfft(lax.optimization_barrier(jnp.sum(piece_freq * jnp.conj(local_freq), axis=1)), n=nwin, axis=-1)[:, :DTLAG]
        centre = piece[:, :, half:half + W]
        piece_mean = lax.optimization_barrier(jnp.mean(centre * centre, axis=(1, 2)))
        outs.append(lagged / jnp.sqrt(3 * W * (local_mean[:, None] + 1e-06) * (piece_mean[:, None] + 1e-06)))
    diffcc = jnp.stack(outs, axis=1)
    return (stack, diffcc)
```

```python
import functools
import math

import jax
import jax.numpy as jnp
import ml_dtypes
import numpy as np
from jax import lax
from jax.experimental import pallas as pl
from jax.experimental.pallas import tpu as pltpu
from jax.sharding import PartitionSpec as P

B = 128
TB = 4
SB = 12
LB = 8
ROWS = 6 * SB
DET = 64
WIN = 256
HALF = 64
EPS = 1e-06
CHUNK = 8
F32 = jnp.float32
BF16 = jnp.bfloat16


def parts(matrix):
    high = matrix.astype(ml_dtypes.bfloat16)
    low = (matrix - high.astype(np.float64)).astype(ml_dtypes.bfloat16)
    return high, low


def tables():
    turns = (np.arange(B)[:, None] * (4 * np.arange(B)[None, :] + 1)) % (4 * B)
    angle = turns * (np.pi / (2 * B))
    forward = np.concatenate(parts(np.concatenate([np.cos(angle), -np.sin(angle)], axis=1)), axis=0)
    back = np.concatenate([np.cos(angle.T), -np.sin(angle.T)], axis=0) / B
    inverse = np.concatenate(parts(back), axis=1)
    n, q = np.arange(B)[:, None], np.arange(B)[None, :]
    ends = np.concatenate([n >= q, n < q], axis=1).astype(ml_dtypes.bfloat16)
    return forward, inverse, np.concatenate([ends, ends], axis=0)


def split(value):
    high = value.astype(BF16)
    return high, (value - high.astype(F32)).astype(BF16)


def dot(a, b):
    return jnp.dot(a, b, preferred_element_type=F32)


def up(value, steps):
    return pltpu.roll(value, value.shape[0] - steps, 0)


def transform(rows, forward):
    out = dot(jnp.concatenate([rows, rows], axis=1), forward)
    return out[:, :B], out[:, B:]


def inverse_dot(real, imag, inverse):
    high, low = split(jnp.concatenate([real, imag], axis=1))
    main = dot(high, inverse)
    return main[:, :B] + main[:, B:] + dot(low, inverse[:, :B])


def kernel(sizes, gx_name, gy_name, st, packed, own, partner, data, tiles, fwd, inv, ends, stack, diff,
           xr, xi, wb, rw, pb, zb, sb, xf, pw, lw, lr, li):
    ngx, ngy = sizes
    groups = ngx * ngy
    gx, gy = lax.axis_index(gx_name), lax.axis_index(gy_name)
    me = gx * ngy + gy
    forward = fwd[...]

    def station_step(i, carry):
        x = data[pl.ds(i * CHUNK, CHUNK)].astype(F32)
        real, imag = transform(x.reshape(CHUNK * ROWS, B).astype(BF16), forward)
        at = pl.ds(pl.multiple_of(i * CHUNK * ROWS, CHUNK * ROWS), CHUNK * ROWS)
        xr[at, :] = real + up(imag, 1)
        xi[at, :] = imag - up(real, 1)
        sq = x * x
        third = ROWS // 3
        energy = sq[:, :third] + sq[:, third : 2 * third] + sq[:, 2 * third :]
        high, low = split(energy.reshape(CHUNK * third, B))
        sums = dot(jnp.concatenate([high, low], axis=1), ends[...])
        one = sums[:, :B] + up(sums[:, B:], 1)
        two = one + up(one, 1)
        four = two + up(two, 2)
        rw[pl.ds(pl.multiple_of(i * CHUNK * third, CHUNK * third), CHUNK * third), :] = lax.rsqrt(
            four * (1.0 / (3 * TB * B)) + EPS
        )
        return carry

    lax.fori_loop(0, groups // CHUNK, station_step, 0)

    count = tiles.shape[0]
    square = jnp.zeros((count, B), F32)
    for b in range(3 * TB):
        t = tiles[:, b * B : (b + 1) * B].astype(F32)
        square = square + t * t
    mean = jnp.sum(square, axis=1, keepdims=True) * (1.0 / (3 * TB * B))
    scale = lax.rsqrt((3 * TB * B) * (mean + EPS))
    for b in range(3 * TB):
        real, imag = transform(tiles[:, b * B : (b + 1) * B], forward)
        wb[2 * b] = real * scale
        wb[2 * b + 1] = imag * scale

    slots = st.shape[1]
    templates = st.shape[0]

    def product_step(i, carry):
        for k in range(slots):
            s = st[i, k]
            base = lax.div(s, 2) * ROWS + lax.rem(s, 2) * SB
            row = i * slots + k
            real = jnp.zeros((LB, B), F32)
            imag = jnp.zeros((LB, B), F32)
            for c in range(3):
                for a in range(TB):
                    at = pl.ds(base + c * 2 * SB + a, LB)
                    x_re, x_im = xr[at, :], xi[at, :]
                    w_re = wb[2 * (c * TB + a), pl.ds(row, 1), :]
                    w_im = wb[2 * (c * TB + a) + 1, pl.ds(row, 1), :]
                    real = real + x_re * w_re + x_im * w_im
                    imag = imag + x_im * w_re - x_re * w_im
            at = pl.ds(pl.multiple_of(row * LB, LB), LB)
            pb[at, :B] = real
            pb[at, B:] = imag
        return carry

    lax.fori_loop(0, templates, product_step, 0)

    def back_step(i, carry):
        size = 8 * slots * LB
        part = pb[pl.ds(pl.multiple_of(i * size, size), size), :]
        zb[pl.ds(pl.multiple_of(i * size, size), size), :] = inverse_dot(part[:, :B], part[:, B:], inv[...])
        return carry

    lax.fori_loop(0, templates // 8, back_step, 0)

    def stack_step(i, carry):
        total = jnp.zeros((LB, B), F32)
        for k in range(slots):
            s = st[i, k]
            z = zb[pl.ds(pl.multiple_of((i * slots + k) * LB, LB), LB), :]
            total = total + z * rw[pl.ds(s * SB, LB), :]
        sb[pl.ds(pl.multiple_of(i * LB, LB), LB), :] = total * (1.0 / math.sqrt(slots))
        return carry

    lax.fori_loop(0, templates, stack_step, 0)
    for p in range(LB):
        stack[:, p * B : (p + 1) * B] = sb[pl.ds(p, templates, stride=LB), :]

    moves = ((1, 0), (-1, 0), (0, 1), (0, -1))
    valid = []
    for d, (dx, dy) in enumerate(moves):
        nx, ny = gx + dx, gy + dy
        inside = (nx >= 0) & (nx < ngx) & (ny >= 0) & (ny < ngy)
        valid.append(jnp.where(inside, 1.0, 0.0).astype(F32))
        there = jnp.where(inside, nx * ngy + ny, me)
        xf[d * ROWS : (d + 1) * ROWS] = data[there].astype(F32)
    xf[4 * ROWS : 5 * ROWS] = data[me].astype(F32)
    xf[5 * ROWS :] = jnp.zeros((xf.shape[0] - 5 * ROWS, B), F32)
    lane = lax.broadcasted_iota(jnp.int32, (8, B), 1)

    def window(which, station, start, c):
        block, offset = lax.div(start, B), lax.rem(start, B)
        base = which * ROWS + c * 2 * SB + station * SB + block
        shift = lax.rem(B - offset, B)
        first = pltpu.roll(xf[pl.ds(base, 8), :], shift, 1)
        second = pltpu.roll(xf[pl.ds(base + 1, 8), :], shift, 1)
        return jnp.where(lane < B - offset, first, second)

    def cut_step(e, carry):
        at = pl.ds(pl.multiple_of(e * 4, 4), 8)
        mine = own[e]
        for c in range(3):
            lw[c, at, :] = window(4, lax.div(mine, 2048), lax.rem(mine, 2048), c)
        for d in range(4):
            other = packed[d, partner[e, d]]
            for c in range(3):
                pw[c * 4 + d, at, :] = window(d, lax.div(other, 2048), lax.rem(other, 2048) - HALF, c)
        return carry

    lax.fori_loop(0, DET, cut_step, 0)

    size = 4 * DET
    row_of = lax.rem(lax.broadcasted_iota(jnp.int32, (size, B), 0), 4)
    lane_of = lax.broadcasted_iota(jnp.int32, (size, B), 1)

    def mean_of(square, mask):
        total = jnp.sum(jnp.where(mask, square, 0.0), axis=1, keepdims=True)
        zb[0:size, :] = jnp.broadcast_to(total, (size, B))
        out = zb[pl.ds(0, DET, stride=4), :]
        for r in range(1, 3):
            out = out + zb[pl.ds(r, DET, stride=4), :]
        return out * (1.0 / (3 * WIN))

    square = jnp.zeros((size, B), F32)
    for c in range(3):
        rows = lw[c, 0:size, :]
        square = square + rows * rows
        real, imag = transform(rows.astype(BF16), forward)
        lr[c] = real
        li[c] = imag
    local_scale = lax.rsqrt((3 * WIN) * (mean_of(square, row_of < 2) + EPS))
    centre = ((row_of == 0) & (lane_of >= HALF)) | (row_of == 1) | ((row_of == 2) & (lane_of < HALF))
    for d in range(4):
        square = jnp.zeros((size, B), F32)
        out_re = jnp.zeros((size, B), F32)
        out_im = jnp.zeros((size, B), F32)
        for c in range(3):
            rows = pw[c * 4 + d, 0:size, :]
            square = square + rows * rows
            real, imag = transform(rows.astype(BF16), forward)
            x_re = real + up(imag, 1)
            x_im = imag - up(real, 1)
            w_re, w_im = lr[c], li[c]
            out_re = out_re + x_re * w_re + x_im * w_im
            out_im = out_im + x_im * w_re - x_re * w_im
        piece_scale = lax.rsqrt(mean_of(square, centre) + EPS)
        zb[0:size, :] = inverse_dot(out_re, out_im, inv[...])
        raw = zb[pl.ds(0, DET, stride=4), :] + zb[pl.ds(1, DET, stride=4), :]
        diff[pl.ds(d, DET, stride=4), :] = raw * local_scale * piece_scale * valid[d]


def on_device(waveforms, templates, tpl_stations, det_station, det_time, partner):
    ngx, ngy = lax.axis_size("gx"), lax.axis_size("gy")
    groups = ngx * ngy
    count = templates.shape[0] * templates.shape[1]
    rows = jnp.transpose(waveforms, (1, 0, 2)).reshape(1, ROWS, B)
    data = lax.all_gather(rows, ("gx", "gy"), axis=0, tiled=True)
    own = det_station * 2048 + det_time

    def from_behind(value, axis, steps):
        size = lax.axis_size(axis)
        pairs = [(i, i + steps) for i in range(max(0, -steps), min(size, size - steps))]
        return lax.ppermute(value, axis, pairs)

    packed = jnp.stack([from_behind(own, "gx", -1), from_behind(own, "gx", 1),
                        from_behind(own, "gy", -1), from_behind(own, "gy", 1)])
    packed = jnp.where((packed & 2047) < HALF, HALF, packed)
    forward, inverse, ends = tables()
    smem = pl.BlockSpec(memory_space=pltpu.SMEM)
    vmem = pl.BlockSpec(memory_space=pltpu.VMEM)
    stack, diff = pl.pallas_call(
        functools.partial(kernel, (ngx, ngy), "gx", "gy"),
        out_shape=(
            jax.ShapeDtypeStruct((templates.shape[0], LB * B), F32),
            jax.ShapeDtypeStruct((4 * DET, B), F32),
        ),
        in_specs=[smem] * 4 + [vmem] * 5,
        out_specs=(vmem, vmem),
        scratch_shapes=[
            pltpu.VMEM((groups * ROWS, B), F32),
            pltpu.VMEM((groups * ROWS, B), F32),
            pltpu.VMEM((6 * TB, count, B), F32),
            pltpu.VMEM((groups * 2 * SB, B), F32),
            pltpu.VMEM((count * LB, 2 * B), F32),
            pltpu.VMEM((count * LB, B), F32),
            pltpu.VMEM((templates.shape[0] * LB, B), F32),
            pltpu.VMEM((5 * ROWS + 16, B), F32),
            pltpu.VMEM((12, 4 * DET + 8, B), F32),
            pltpu.VMEM((3, 4 * DET + 8, B), F32),
            pltpu.VMEM((3, 4 * DET, B), F32),
            pltpu.VMEM((3, 4 * DET, B), F32),
        ],
        compiler_params=pltpu.CompilerParams(vmem_limit_bytes=60 * 1024 * 1024),
    )(tpl_stations, packed, own, partner, data, templates.reshape(count, 3 * TB * B),
      jnp.asarray(forward), jnp.asarray(inverse), jnp.asarray(ends))
    return stack, diff.reshape(DET, 4, B)


def solution(mesh):
    return jax.shard_map(
        on_device,
        mesh=mesh,
        in_specs=(
            P(("gx", "gy"), None, None),
            P(("gx", "gy"), None, None),
            P(("gx", "gy"), None),
            P(("gx", "gy")),
            P(("gx", "gy")),
            P(("gx", "gy"), None),
        ),
        out_specs=(P(("gx", "gy"), None), P(("gx", "gy"), None, None)),
        check_vma=False,
    )
```

```python
import functools
import math

import jax
import jax.numpy as jnp
import ml_dtypes
import numpy as np
from jax import lax
from jax.experimental import pallas as pl
from jax.experimental.pallas import tpu as pltpu
from jax.sharding import PartitionSpec as P

B = 128
TB = 4
SB = 12
LB = 8
ROWS = 6 * SB
DET = 64
WIN = 256
HALF = 64
EPS = 1e-06
CHUNK = 8
F32 = jnp.float32
BF16 = jnp.bfloat16


def parts(matrix):
    high = matrix.astype(ml_dtypes.bfloat16)
    low = (matrix - high.astype(np.float64)).astype(ml_dtypes.bfloat16)
    return high, low


def tables():
    turns = (np.arange(B)[:, None] * (4 * np.arange(B)[None, :] + 1)) % (4 * B)
    angle = turns * (np.pi / (2 * B))
    forward = np.concatenate(parts(np.concatenate([np.cos(angle), -np.sin(angle)], axis=1)), axis=0)
    back = np.concatenate([np.cos(angle.T), -np.sin(angle.T)], axis=0) / B
    inverse = np.concatenate(parts(back), axis=1)
    n, q = np.arange(B)[:, None], np.arange(B)[None, :]
    ends = np.concatenate([n >= q, n < q], axis=1).astype(ml_dtypes.bfloat16)
    return forward, inverse, np.concatenate([ends, ends], axis=0)


def split(value):
    high = value.astype(BF16)
    return high, (value - high.astype(F32)).astype(BF16)


def dot(a, b):
    return jnp.dot(a, b, preferred_element_type=F32)


def up(value, steps):
    return pltpu.roll(value, value.shape[0] - steps, 0)


def transform(rows, forward):
    out = dot(jnp.concatenate([rows, rows], axis=1), forward)
    return out[:, :B], out[:, B:]


def inverse_dot(real, imag, inverse):
    high, low = split(jnp.concatenate([real, imag], axis=1))
    main = dot(high, inverse)
    return main[:, :B] + main[:, B:] + dot(low, inverse[:, :B])


def ring_layout(ngx, ngy):
    nx = math.isqrt(ngx)
    return {"y": ngx // nx, "x": nx, "z": ngy // 2, "core": 2}


ORDERS = (("x", "y", "z"), ("y", "z", "x"), ("z", "x", "y"))


def gather_kernel(sizes, wave, stations, times, data, words, rows, mine, send_sem, recv_sem, word_sem):
    ngx, ngy = sizes
    dims = ring_layout(ngx, ngy)
    gx, gy = lax.axis_index("gx"), lax.axis_index("gy")
    here = {"y": gx // dims["x"], "x": gx % dims["x"], "z": gy // 2, "core": gy % 2}

    def device(coords):
        return (coords["y"] * dims["x"] + coords["x"], coords["z"] * 2 + coords["core"])

    def moved(axis, steps):
        return {**here, axis: (here[axis] + steps + dims[axis]) % dims[axis]}

    near = (
        ((gx + 1) % ngx, gy),
        ((gx + ngx - 1) % ngx, gy),
        (gx, (gy + 1) % ngy),
        (gx, (gy + ngy - 1) % ngy),
    )
    peers = [device(moved(axis, r)) for axis in ("x", "y", "z") for r in range(1, dims[axis])]
    peers = peers + [device(moved("core", 1))] + list(near)
    barrier = pltpu.get_barrier_semaphore()
    for peer in peers:
        pl.semaphore_signal(barrier, inc=1, device_id=peer, device_id_type=pl.DeviceIdType.MESH)

    for c in range(3):
        value = wave[c].astype(F32)
        for b in range(SB):
            rows[c, pl.ds(b, 2, stride=SB), :] = value[:, b * B : (b + 1) * B]
        data[here["y"], here["x"], here["z"], here["core"], c] = rows[c].astype(BF16)
    mine[...] = jnp.zeros_like(mine)
    mine[:, 0:DET] = stations[...] * 2048 + times[...]
    pl.semaphore_wait(barrier, len(peers))

    started = []

    def send(source, target, to, send_at, recv_at):
        copy = pltpu.make_async_remote_copy(
            src_ref=source, dst_ref=target, send_sem=send_at, recv_sem=recv_at,
            device_id=to, device_id_type=pl.DeviceIdType.MESH)
        copy.start()
        started.append(copy)
        return copy

    def block(coords, whole, c):
        at = tuple(slice(None) if axis in whole else coords[axis] for axis in ("y", "x", "z", "core"))
        return data.at[at + (c,)]

    def send_block(coords, whole, c, to, index):
        ref = block(coords, whole, c)
        return send(ref, ref, to, send_sem.at[c, index], recv_sem.at[c, index])

    arriving = {c: [] for c in range(3)}
    for phase in range(3):
        for c, order in enumerate(ORDERS):
            for copy in arriving[c]:
                copy.wait_recv()
            axis = order[phase]
            arriving[c] = [
                send_block(here, order[:phase], c, device(moved(axis, r)), 3 * phase + r - 1)
                for r in range(1, dims[axis])
            ]
        if phase == 0:
            word_copies = [
                send(mine, words.at[d ^ 1], near[d], word_sem.at[0, d], word_sem.at[1, d ^ 1]) for d in range(4)
            ]
    sibling = device(moved("core", 1))
    last = []
    for c, order in enumerate(ORDERS):
        last.append(send_block(here, order[:2], c, sibling, 9))
    for r in range(1, 4):
        for c, order in enumerate(ORDERS):
            if r < dims[order[2]]:
                arriving[c][r - 1].wait_recv()
                came = moved(order[2], -r)
                last.append(send_block(came, order[:2], c, sibling, 9 + r))
    for copy in last + word_copies:
        copy.wait_recv()
    for copy in started:
        copy.wait_send()


def kernel(sizes, gx_name, gy_name, st, packed, stations, times, partner, data, tiles, fwd, inv, ends, stack, diff,
           xr, xi, wb, rw, pb, zb, sb, xf, pw, lw, lr, li):
    ngx, ngy = sizes
    groups = ngx * ngy
    gx, gy = lax.axis_index(gx_name), lax.axis_index(gy_name)
    me = gx * ngy + gy
    forward = fwd[...]

    def station_step(i, carry):
        x = data[pl.ds(i * CHUNK, CHUNK)].astype(F32).reshape(CHUNK, ROWS, B)
        real, imag = transform(x.reshape(CHUNK * ROWS, B).astype(BF16), forward)
        at = pl.ds(pl.multiple_of(i * CHUNK * ROWS, CHUNK * ROWS), CHUNK * ROWS)
        xr[at, :] = real + up(imag, 1)
        xi[at, :] = imag - up(real, 1)
        sq = x * x
        third = ROWS // 3
        energy = sq[:, :third] + sq[:, third : 2 * third] + sq[:, 2 * third :]
        high, low = split(energy.reshape(CHUNK * third, B))
        sums = dot(jnp.concatenate([high, low], axis=1), ends[...])
        one = sums[:, :B] + up(sums[:, B:], 1)
        two = one + up(one, 1)
        four = two + up(two, 2)
        rw[pl.ds(pl.multiple_of(i * CHUNK * third, CHUNK * third), CHUNK * third), :] = lax.rsqrt(
            four * (1.0 / (3 * TB * B)) + EPS
        )
        return carry

    lax.fori_loop(0, groups // CHUNK, station_step, 0)

    count = tiles.shape[0]
    square = jnp.zeros((count, B), F32)
    for b in range(3 * TB):
        t = tiles[:, b * B : (b + 1) * B].astype(F32)
        square = square + t * t
    mean = jnp.sum(square, axis=1, keepdims=True) * (1.0 / (3 * TB * B))
    scale = lax.rsqrt((3 * TB * B) * (mean + EPS))
    for b in range(3 * TB):
        real, imag = transform(tiles[:, b * B : (b + 1) * B], forward)
        wb[2 * b] = real * scale
        wb[2 * b + 1] = imag * scale

    slots, templates = st.shape

    def product_step(i, carry):
        for k in range(slots):
            s = st[k, i]
            base = lax.div(s, 2) * ROWS + lax.rem(s, 2) * SB
            row = i * slots + k
            real = jnp.zeros((LB, B), F32)
            imag = jnp.zeros((LB, B), F32)
            for c in range(3):
                for a in range(TB):
                    at = pl.ds(base + c * 2 * SB + a, LB)
                    x_re, x_im = xr[at, :], xi[at, :]
                    w_re = wb[2 * (c * TB + a), pl.ds(row, 1), :]
                    w_im = wb[2 * (c * TB + a) + 1, pl.ds(row, 1), :]
                    real = real + x_re * w_re + x_im * w_im
                    imag = imag + x_im * w_re - x_re * w_im
            at = pl.ds(pl.multiple_of(row * LB, LB), LB)
            pb[at, :B] = real
            pb[at, B:] = imag
        return carry

    lax.fori_loop(0, templates, product_step, 0)

    def back_step(i, carry):
        size = 8 * slots * LB
        part = pb[pl.ds(pl.multiple_of(i * size, size), size), :]
        zb[pl.ds(pl.multiple_of(i * size, size), size), :] = inverse_dot(part[:, :B], part[:, B:], inv[...])
        return carry

    lax.fori_loop(0, templates // 8, back_step, 0)

    def stack_step(i, carry):
        total = jnp.zeros((LB, B), F32)
        for k in range(slots):
            s = st[k, i]
            z = zb[pl.ds(pl.multiple_of((i * slots + k) * LB, LB), LB), :]
            total = total + z * rw[pl.ds(s * SB, LB), :]
        sb[pl.ds(pl.multiple_of(i * LB, LB), LB), :] = total * (1.0 / math.sqrt(slots))
        return carry

    lax.fori_loop(0, templates, stack_step, 0)
    for p in range(LB):
        stack[:, p * B : (p + 1) * B] = sb[pl.ds(p, templates, stride=LB), :]

    moves = ((1, 0), (-1, 0), (0, 1), (0, -1))
    valid = []
    for d, (dx, dy) in enumerate(moves):
        nx, ny = gx + dx, gy + dy
        inside = (nx >= 0) & (nx < ngx) & (ny >= 0) & (ny < ngy)
        valid.append(jnp.where(inside, 1.0, 0.0).astype(F32))
        there = jnp.where(inside, nx * ngy + ny, me)
        xf[d * ROWS : (d + 1) * ROWS] = data[there].astype(F32).reshape(ROWS, B)
    xf[4 * ROWS : 5 * ROWS] = data[me].astype(F32).reshape(ROWS, B)
    xf[5 * ROWS :] = jnp.zeros((xf.shape[0] - 5 * ROWS, B), F32)
    lane = lax.broadcasted_iota(jnp.int32, (8, B), 1)

    def window(which, station, start, c):
        block, offset = lax.div(start, B), lax.rem(start, B)
        base = which * ROWS + c * 2 * SB + station * SB + block
        shift = lax.rem(B - offset, B)
        first = pltpu.roll(xf[pl.ds(base, 8), :], shift, 1)
        second = pltpu.roll(xf[pl.ds(base + 1, 8), :], shift, 1)
        return jnp.where(lane < B - offset, first, second)

    def cut_step(e, carry):
        at = pl.ds(pl.multiple_of(e * 4, 4), 8)
        mine = stations[e] * 2048 + times[e]
        for c in range(3):
            lw[c, at, :] = window(4, lax.div(mine, 2048), lax.rem(mine, 2048), c)
        for d in range(4):
            other = packed[d, partner[d, e]]
            for c in range(3):
                pw[c * 4 + d, at, :] = window(d, lax.div(other, 2048), lax.rem(other, 2048) - HALF, c)
        return carry

    lax.fori_loop(0, DET, cut_step, 0)

    size = 4 * DET
    row_of = lax.rem(lax.broadcasted_iota(jnp.int32, (size, B), 0), 4)
    lane_of = lax.broadcasted_iota(jnp.int32, (size, B), 1)

    def mean_of(square, mask):
        total = jnp.sum(jnp.where(mask, square, 0.0), axis=1, keepdims=True)
        zb[0:size, :] = jnp.broadcast_to(total, (size, B))
        out = zb[pl.ds(0, DET, stride=4), :]
        for r in range(1, 3):
            out = out + zb[pl.ds(r, DET, stride=4), :]
        return out * (1.0 / (3 * WIN))

    square = jnp.zeros((size, B), F32)
    for c in range(3):
        rows = lw[c, 0:size, :]
        square = square + rows * rows
        real, imag = transform(rows.astype(BF16), forward)
        lr[c] = real
        li[c] = imag
    local_scale = lax.rsqrt((3 * WIN) * (mean_of(square, row_of < 2) + EPS))
    centre = ((row_of == 0) & (lane_of >= HALF)) | (row_of == 1) | ((row_of == 2) & (lane_of < HALF))
    for d in range(4):
        square = jnp.zeros((size, B), F32)
        out_re = jnp.zeros((size, B), F32)
        out_im = jnp.zeros((size, B), F32)
        for c in range(3):
            rows = pw[c * 4 + d, 0:size, :]
            square = square + rows * rows
            real, imag = transform(rows.astype(BF16), forward)
            x_re = real + up(imag, 1)
            x_im = imag - up(real, 1)
            w_re, w_im = lr[c], li[c]
            out_re = out_re + x_re * w_re + x_im * w_im
            out_im = out_im + x_im * w_re - x_re * w_im
        piece_scale = lax.rsqrt(mean_of(square, centre) + EPS)
        zb[0:size, :] = inverse_dot(out_re, out_im, inv[...])
        raw = zb[pl.ds(0, DET, stride=4), :] + zb[pl.ds(1, DET, stride=4), :]
        diff[pl.ds(d, DET, stride=4), :] = raw * local_scale * piece_scale * valid[d]


def on_device(waveforms, templates, tpl_stations, det_station, det_time, partner):
    ngx, ngy = lax.axis_size("gx"), lax.axis_size("gy")
    groups = ngx * ngy
    count = templates.shape[0] * templates.shape[1]
    smem = pl.BlockSpec(memory_space=pltpu.SMEM)
    vmem = pl.BlockSpec(memory_space=pltpu.VMEM)
    dims = ring_layout(ngx, ngy)
    data, words = pl.pallas_call(
        functools.partial(gather_kernel, (ngx, ngy)),
        out_shape=(
            jax.ShapeDtypeStruct((dims["y"], dims["x"], dims["z"], 2, 3, 2 * SB, B), BF16),
            jax.ShapeDtypeStruct((4, 1, B), jnp.int32),
        ),
        in_specs=[vmem] * 3,
        out_specs=(vmem, vmem),
        scratch_shapes=[
            pltpu.VMEM((3, 2 * SB, B), F32),
            pltpu.VMEM((1, B), jnp.int32),
            pltpu.SemaphoreType.DMA((3, 13)),
            pltpu.SemaphoreType.DMA((3, 13)),
            pltpu.SemaphoreType.DMA((2, 4)),
        ],
        compiler_params=pltpu.CompilerParams(
            collective_id=0, has_side_effects=True, vmem_limit_bytes=16 * 1024 * 1024
        ),
    )(jnp.transpose(waveforms, (1, 0, 2)), det_station.reshape(1, DET), det_time.reshape(1, DET))
    data = data.reshape(groups, 3, 2 * SB, B)
    packed = words.reshape(4, B)
    forward, inverse, ends = tables()
    stack, diff = pl.pallas_call(
        functools.partial(kernel, (ngx, ngy), "gx", "gy"),
        out_shape=(
            jax.ShapeDtypeStruct((templates.shape[0], LB * B), F32),
            jax.ShapeDtypeStruct((4 * DET, B), F32),
        ),
        in_specs=[smem] * 5 + [vmem] * 5,
        out_specs=(vmem, vmem),
        scratch_shapes=[
            pltpu.VMEM((groups * ROWS, B), F32),
            pltpu.VMEM((groups * ROWS, B), F32),
            pltpu.VMEM((6 * TB, count, B), F32),
            pltpu.VMEM((groups * 2 * SB, B), F32),
            pltpu.VMEM((count * LB, 2 * B), F32),
            pltpu.VMEM((count * LB, B), F32),
            pltpu.VMEM((templates.shape[0] * LB, B), F32),
            pltpu.VMEM((5 * ROWS + 16, B), F32),
            pltpu.VMEM((12, 4 * DET + 8, B), F32),
            pltpu.VMEM((3, 4 * DET + 8, B), F32),
            pltpu.VMEM((3, 4 * DET, B), F32),
            pltpu.VMEM((3, 4 * DET, B), F32),
        ],
        compiler_params=pltpu.CompilerParams(vmem_limit_bytes=60 * 1024 * 1024),
    )(tpl_stations.T, packed, det_station, det_time, partner.T, data, templates.reshape(count, 3 * TB * B),
      jnp.asarray(forward), jnp.asarray(inverse), jnp.asarray(ends))
    return stack, diff.reshape(DET, 4, B)


def solution(mesh):
    return jax.shard_map(
        on_device,
        mesh=mesh,
        in_specs=(
            P(("gx", "gy"), None, None),
            P(("gx", "gy"), None, None),
            P(("gx", "gy"), None),
            P(("gx", "gy")),
            P(("gx", "gy")),
            P(("gx", "gy"), None),
        ),
        out_specs=(P(("gx", "gy"), None), P(("gx", "gy"), None, None)),
        check_vma=False,
    )
```

```python
import functools
import math

import jax
import jax.numpy as jnp
import ml_dtypes
import numpy as np
from jax import lax
from jax.experimental import pallas as pl
from jax.experimental.pallas import tpu as pltpu
from jax.sharding import PartitionSpec as P

B = 128
TB = 4
SB = 12
LB = 8
ROWS = 6 * SB
DET = 64
WIN = 256
HALF = 64
EPS = 1e-06
CHUNK = 8
F32 = jnp.float32
BF16 = jnp.bfloat16


def parts(matrix):
    high = matrix.astype(ml_dtypes.bfloat16)
    low = (matrix - high.astype(np.float64)).astype(ml_dtypes.bfloat16)
    return high, low


def tables():
    turns = (np.arange(B)[:, None] * (4 * np.arange(B)[None, :] + 1)) % (4 * B)
    angle = turns * (np.pi / (2 * B))
    forward = np.concatenate(parts(np.concatenate([np.cos(angle), -np.sin(angle)], axis=1)), axis=0)
    back = np.concatenate([np.cos(angle.T), -np.sin(angle.T)], axis=0) / B
    inverse = np.concatenate(parts(back), axis=1)
    n, q = np.arange(B)[:, None], np.arange(B)[None, :]
    ends = np.concatenate([n >= q, n < q], axis=1).astype(ml_dtypes.bfloat16)
    return forward, inverse, np.concatenate([ends, ends], axis=0)


def split(value):
    high = value.astype(BF16)
    return high, (value - high.astype(F32)).astype(BF16)


def dot(a, b):
    return jnp.dot(a, b, preferred_element_type=F32)


def up(value, steps):
    return pltpu.roll(value, value.shape[0] - steps, 0)


def transform(rows, forward):
    out = dot(jnp.concatenate([rows, rows], axis=1), forward)
    return out[:, :B], out[:, B:]


def inverse_dot(real, imag, inverse):
    high, low = split(jnp.concatenate([real, imag], axis=1))
    main = dot(high, inverse)
    return main[:, :B] + main[:, B:] + dot(low, inverse[:, :B])


def ring_layout(ngx, ngy):
    nx = math.isqrt(ngx)
    return {"y": ngx // nx, "x": nx, "z": ngy // 2, "core": 2}


ORDERS = (("x", "y", "z"), ("y", "z", "x"), ("z", "x", "y"))


def kernel(sizes, st, stations, times, partner, wave_in, station_in, time_in, tiles_in, fwd_in, inv_in, ends_in, stack, diff,
           data, near_data, wave, tiles, fwd, inv, ends, rows, station_row, time_row, mine, words, packed,
           xr, xi, wb, rw, pb, sb, xf, pw, lw, lr, li, lq, pq, er, ei, gr, gi,
           send_sem, recv_sem, near_sem, word_sem, load_sem):
    ngx, ngy = sizes
    dims = ring_layout(ngx, ngy)
    groups = ngx * ngy
    gx, gy = lax.axis_index("gx"), lax.axis_index("gy")
    here = {"y": gx // dims["x"], "x": gx % dims["x"], "z": gy // 2, "core": gy % 2}
    mesh_id = pl.DeviceIdType.MESH
    third = 2 * SB

    def device(coords):
        return (coords["y"] * dims["x"] + coords["x"], coords["z"] * 2 + coords["core"])

    def linear(coords):
        return ((coords["y"] * dims["x"] + coords["x"]) * dims["z"] + coords["z"]) * 2 + coords["core"]

    def moved(axis, steps):
        return {**here, axis: (here[axis] + steps + dims[axis]) % dims[axis]}

    loads = []
    for i, (source, target) in enumerate(
        ((wave_in, wave), (station_in, station_row), (time_in, time_row), (fwd_in, fwd), (tiles_in, tiles),
         (inv_in, inv), (ends_in, ends))
    ):
        copy = pltpu.make_async_copy(source, target, load_sem.at[i])
        copy.start()
        loads.append(copy)

    near = (
        ((gx + 1) % ngx, gy),
        ((gx + ngx - 1) % ngx, gy),
        (gx, (gy + 1) % ngy),
        (gx, (gy + ngy - 1) % ngy),
    )
    sibling = device(moved("core", 1))
    peers = [device(moved(axis, r)) for axis in ("x", "y", "z") for r in range(1, dims[axis])]
    peers = peers + [sibling] + list(near)
    barrier = pltpu.get_barrier_semaphore()
    for peer in peers:
        pl.semaphore_signal(barrier, inc=1, device_id=peer, device_id_type=mesh_id)

    loads[0].wait()
    for c in range(3):
        value = wave[c].astype(F32)
        for b in range(SB):
            rows[c, pl.ds(b, 2, stride=SB), :] = value[:, b * B : (b + 1) * B]
        data[here["y"], here["x"], here["z"], here["core"], c] = rows[c].astype(BF16)
    loads[1].wait()
    loads[2].wait()
    mine[...] = jnp.zeros_like(mine)
    mine[:, 0:DET] = station_row[...] * 2048 + time_row[...]
    pl.semaphore_wait(barrier, len(peers))

    def send(source, target, to, send_at, recv_at):
        return pltpu.make_async_remote_copy(
            src_ref=source, dst_ref=target, send_sem=send_at, recv_sem=recv_at, device_id=to, device_id_type=mesh_id)

    def place(coords, whole):
        return tuple(slice(None) if axis in whole else coords[axis] for axis in ("y", "x", "z", "core"))

    def block_copy(coords, whole, c, to, index):
        ref = data.at[place(coords, whole) + (c,)]
        return send(ref, ref, to, send_sem.at[c, index], recv_sem.at[c, index])

    def phase_copy(c, phase, r):
        order = ORDERS[c]
        return block_copy(here, order[:phase], c, device(moved(order[phase], r)), 3 * phase + r - 1)

    def steps(c, phase):
        count = dims[ORDERS[c][phase]]
        return [r for r in (1, 3, 2) if r < count]

    def start_phase(phase):
        for c in range(3):
            if phase:
                for r in steps(c, phase - 1):
                    phase_copy(c, phase - 1, r).wait_recv()
            for r in steps(c, phase):
                phase_copy(c, phase, r).start()

    def plane_copy(c, r):
        return block_copy(moved(ORDERS[c][2], -r), ORDERS[c][:2], c, sibling, 9 + r)

    start_phase(0)
    own_block = data.at[place(here, ()) + (slice(None),)]
    near_copies = []
    for d in range(4):
        near_copies.append(send(mine, words.at[d ^ 1], near[d], word_sem.at[0, d], word_sem.at[1, d ^ 1]))
        near_copies.append(send(own_block, near_data.at[d ^ 1], near[d], near_sem.at[0, d], near_sem.at[1, d ^ 1]))
    for copy in near_copies:
        copy.start()

    for copy in loads[3:]:
        copy.wait()
    forward = fwd[...]
    count = tiles.shape[0]
    square = jnp.zeros((count, B), F32)
    for b in range(3 * TB):
        t = tiles[:, b * B : (b + 1) * B].astype(F32)
        square = square + t * t
    mean = jnp.sum(square, axis=1, keepdims=True) * (1.0 / (3 * TB * B))
    scale = lax.rsqrt((3 * TB * B) * (mean + EPS))
    for b in range(3 * TB):
        real, imag = transform(tiles[:, b * B : (b + 1) * B], forward)
        wb[2 * b] = real * scale
        wb[2 * b + 1] = imag * scale

    start_phase(1)

    moves = ((1, 0), (-1, 0), (0, 1), (0, -1))
    span = 2 * SB
    xf[...] = jnp.zeros_like(xf)
    flat = xf.reshape(8 * xf.shape[0], B)
    valid = []
    for copy in near_copies:
        copy.wait_recv()
    to_scalars = pltpu.make_async_copy(words, packed, load_sem.at[7])
    to_scalars.start()
    for d, (dx, dy) in enumerate(moves + ((0, 0),)):
        nx, ny = gx + dx, gy + dy
        inside = (nx >= 0) & (nx < ngx) & (ny >= 0) & (ny < ngy)
        valid.append(jnp.where(inside, 1.0, 0.0).astype(F32))
        x = (near_data[d] if d < 4 else data[place(here, ())]).astype(F32)
        for c in range(3):
            flat[pl.ds((1 + d * span) * 8 + c, span, stride=8), :] = x[c]
            flat[pl.ds(d * span * 8 + 4 + c, span, stride=8), :] = x[c]
    to_scalars.wait()
    lane = lax.broadcasted_iota(jnp.int32, (8, B), 1)
    upper = lax.broadcasted_iota(jnp.int32, (8, B), 0) < 4
    mask_first = jnp.where(upper & (lane < HALF), 0.0, 1.0).astype(F32)
    mask_last = jnp.where(upper | (lane >= HALF), 0.0, 1.0).astype(F32)

    def window(which, station, start, blocks):
        block, offset = lax.shift_right_logical(start, 7), lax.bitwise_and(start, B - 1)
        base = 1 + which * span + station * SB + block
        shift = lax.bitwise_and(B - offset, B - 1)
        inner = lane < B - offset
        turned = [pltpu.roll(xf[base + j], shift, 1) for j in range(blocks)]
        return [jnp.where(inner, turned[j], turned[j + 1]) for j in range(blocks - 1)]

    def cut_step(e, carry):
        at = pl.ds(pl.multiple_of(e * 8, 8), 8)
        (first,) = window(4, stations[e], times[e], 2)
        lw[at, :] = first
        lq[at, :] = first * first
        for d in range(4):
            word = packed[d, 0, partner[d, e]]
            start = jnp.maximum(lax.bitwise_and(word, 2047) - HALF, 0)
            first, second = window(d, lax.shift_right_logical(word, 11), start, 3)
            pw[d, pl.ds(pl.multiple_of(e * 12, 4), 8), :] = first
            pw[d, pl.ds(pl.multiple_of(e * 12 + 4, 4), 8), :] = second
            pq[d, at, :] = first * first * mask_first + second * second * mask_last
        return carry

    lax.fori_loop(0, DET, cut_step, 0, unroll=4)

    start_phase(2)
    for c in range(3):
        plane_copy(c, 0).start()

    lr[...], li[...] = transform(lw[...].astype(BF16), forward)
    for d in range(4):
        er[d], ei[d] = transform(pw[d].astype(BF16), forward)

    def pair_step(e, carry):
        at = pl.ds(pl.multiple_of(e * 8, 8), 8)
        low, high = pl.ds(pl.multiple_of(e * 12, 4), 8), pl.ds(pl.multiple_of(e * 12 + 4, 4), 8)
        w_re, w_im = lr[at, :], li[at, :]
        for d in range(4):
            x_re = er[d, low, :] + ei[d, high, :]
            x_im = ei[d, low, :] - er[d, high, :]
            gr[d, at, :] = x_re * w_re + x_im * w_im
            gi[d, at, :] = x_im * w_re - x_re * w_im
        return carry

    lax.fori_loop(0, DET, pair_step, 0, unroll=2)

    def gathered(ref, *lead):
        out = ref[lead + (pl.ds(0, DET, stride=8),)]
        for r in range(1, 8):
            out = out + ref[lead + (pl.ds(r, DET, stride=8),)]
        return out

    def mean_of(ref, *lead):
        return jnp.sum(gathered(ref, *lead), axis=1, keepdims=True) * (1.0 / (3 * WIN))

    local_scale = lax.rsqrt((3 * WIN) * (mean_of(lq) + EPS))
    for d in range(4):
        raw = inverse_dot(gathered(gr, d), gathered(gi, d), inv[...])
        scale = local_scale * lax.rsqrt(mean_of(pq, d) + EPS) * valid[d]
        diff[pl.ds(d, DET, stride=4), :] = raw * scale

    def transform_plane(c, coords):
        order = ORDERS[c]
        inner = [axis for axis in ("y", "x", "z") if axis in order[:2]]
        size = dims[inner[0]] * dims[inner[1]]
        x = data[place(coords, order[:2]) + (c,)].astype(F32).reshape(size * third, B)
        real, imag = transform(x.astype(BF16), forward)
        w_re, w_im = real + up(imag, 1), imag - up(real, 1)
        for i in range(size):
            full = {**coords, inner[0]: i // dims[inner[1]], inner[1]: i % dims[inner[1]]}
            for sta in range(2):
                at = 2 * (c * groups + linear(full)) + sta
                begin = i * third + sta * SB
                xr[at, 0:SB] = w_re[begin : begin + SB]
                xi[at, 0:SB] = w_im[begin : begin + SB]

    def energy(core):
        def step(y, carry):
            size = dims["x"] * dims["z"]
            x = data[y, :, :, core].astype(F32)
            sq = x * x
            total = (sq[:, :, 0] + sq[:, :, 1] + sq[:, :, 2]).reshape(size * third, B)
            high, low = split(total)
            sums = dot(jnp.concatenate([high, low], axis=1), ends[...])
            one = sums[:, :B] + up(sums[:, B:], 1)
            two = one + up(one, 1)
            four = two + up(two, 2)
            out = lax.rsqrt(four * (1.0 / (3 * TB * B)) + EPS)
            for i in range(size):
                full = {"y": y, "x": i // dims["z"], "z": i % dims["z"], "core": core}
                for sta in range(2):
                    begin = i * third + sta * SB
                    rw[2 * linear(full) + sta] = out[begin : begin + LB]
            return carry

        lax.fori_loop(0, dims["y"], step, 0)

    side = dims["z"]

    def turn(o):
        return o + (o // 2) * (1 - 2 * (o % 2))

    def own_step(o, carry):
        r = turn(o)
        for c in range(3):
            @pl.when(o > 0)
            def _():
                block_copy(here, ORDERS[c][:2], c, device(moved(ORDERS[c][2], r)), 5 + r).wait_recv()
                plane_copy(c, r).start()
        for c in range(3):
            transform_plane(c, moved(ORDERS[c][2], -r))
        return carry

    lax.fori_loop(0, side, own_step, 0)
    energy(here["core"])

    def other_step(o, carry):
        r = turn(o)
        for c in range(3):
            plane_copy(c, r).wait_recv()
        for c in range(3):
            transform_plane(c, {**moved(ORDERS[c][2], -r), "core": 1 - here["core"]})
        return carry

    lax.fori_loop(0, side, other_step, 0)
    energy(1 - here["core"])

    slots, templates = st.shape

    def product_step(i, carry):
        for k in range(slots):
            s = st[k, i]
            row = i * slots + k
            real = jnp.zeros((LB, B), F32)
            imag = jnp.zeros((LB, B), F32)
            for c in range(3):
                all_re, all_im = xr[s + 2 * c * groups], xi[s + 2 * c * groups]
                for a in range(TB):
                    x_re, x_im = all_re[a : a + LB], all_im[a : a + LB]
                    w_re = wb[2 * (c * TB + a), pl.ds(row, 1), :]
                    w_im = wb[2 * (c * TB + a) + 1, pl.ds(row, 1), :]
                    real = real + x_re * w_re + x_im * w_im
                    imag = imag + x_im * w_re - x_re * w_im
            at = pl.ds(pl.multiple_of(row * LB, LB), LB)
            pb[at, :B] = real
            pb[at, B:] = imag
        return carry

    lax.fori_loop(0, templates, product_step, 0)
    group = 2

    def back_step(i, carry):
        size = group * slots * LB
        part = pb[pl.ds(pl.multiple_of(i * size, size), size), :]
        z = inverse_dot(part[:, :B], part[:, B:], inv[...])
        for j in range(group):
            total = jnp.zeros((LB, B), F32)
            for k in range(slots):
                s = st[k, i * group + j]
                row = (j * slots + k) * LB
                total = total + z[row : row + LB] * rw[s]
            sb[pl.ds(pl.multiple_of((i * group + j) * LB, LB), LB), :] = total * (1.0 / math.sqrt(slots))
        return carry

    lax.fori_loop(0, templates // group, back_step, 0, unroll=2)
    for p in range(LB):
        stack[:, p * B : (p + 1) * B] = sb[pl.ds(p, templates, stride=LB), :]

    for copy in near_copies:
        copy.wait_send()
    for c in range(3):
        for phase in range(3):
            for r in steps(c, phase):
                phase_copy(c, phase, r).wait_send()
        for r in range(side):
            plane_copy(c, r).wait_send()


def on_device(waveforms, templates, tpl_stations, det_station, det_time, partner):
    ngx, ngy = lax.axis_size("gx"), lax.axis_size("gy")
    groups = ngx * ngy
    count = templates.shape[0] * templates.shape[1]
    forward, inverse, ends = tables()
    smem = pl.BlockSpec(memory_space=pltpu.SMEM)
    vmem = pl.BlockSpec(memory_space=pltpu.VMEM)
    anywhere = pl.BlockSpec(memory_space=pl.ANY)
    dims = ring_layout(ngx, ngy)
    ntpl = templates.shape[0]

    def floats(*shape):
        return pltpu.VMEM(shape, F32)

    def halves(*shape):
        return pltpu.VMEM(shape, BF16)

    def ints(*shape):
        return pltpu.VMEM(shape, jnp.int32)

    stack, diff = pl.pallas_call(
        functools.partial(kernel, (ngx, ngy)),
        out_shape=(
            jax.ShapeDtypeStruct((ntpl, LB * B), F32),
            jax.ShapeDtypeStruct((4 * DET, B), F32),
        ),
        in_specs=[smem] * 4 + [anywhere] * 7,
        out_specs=(vmem, vmem),
        scratch_shapes=[
            halves(dims["y"], dims["x"], dims["z"], 2, 3, 2 * SB, B),
            halves(4, 3, 2 * SB, B),
            halves(3, 2, SB * B),
            halves(count, 3 * TB * B),
            halves(2 * B, 2 * B),
            halves(2 * B, 2 * B),
            halves(2 * B, 2 * B),
            floats(3, 2 * SB, B),
            ints(1, DET),
            ints(1, DET),
            ints(1, B),
            ints(4, 1, B),
            pltpu.SMEM((4, 1, B), jnp.int32),
            floats(groups * 6, 16, B),
            floats(groups * 6, 16, B),
            floats(6 * TB, count, B),
            floats(groups * 2, LB, B),
            floats(count * LB, 2 * B),
            floats(ntpl * LB, B),
            floats(10 * SB + 4, 8, B),
            floats(4, 12 * DET, B),
            floats(8 * DET, B),
            floats(8 * DET, B),
            floats(8 * DET, B),
            floats(8 * DET, B),
            floats(4, 8 * DET, B),
            floats(4, 12 * DET, B),
            floats(4, 12 * DET, B),
            floats(4, 8 * DET, B),
            floats(4, 8 * DET, B),
            pltpu.SemaphoreType.DMA((3, 13)),
            pltpu.SemaphoreType.DMA((3, 13)),
            pltpu.SemaphoreType.DMA((2, 4)),
            pltpu.SemaphoreType.DMA((2, 4)),
            pltpu.SemaphoreType.DMA((8,)),
        ],
        compiler_params=pltpu.CompilerParams(
            collective_id=0, has_side_effects=True, vmem_limit_bytes=60 * 1024 * 1024
        ),
    )(tpl_stations.T, det_station, det_time, partner.T, jnp.transpose(waveforms, (1, 0, 2)),
      det_station.reshape(1, DET), det_time.reshape(1, DET), templates.reshape(count, 3 * TB * B),
      jnp.asarray(forward), jnp.asarray(inverse), jnp.asarray(ends))
    return stack, diff.reshape(DET, 4, B)


def solution(mesh):
    return jax.shard_map(
        on_device,
        mesh=mesh,
        in_specs=(
            P(("gx", "gy"), None, None),
            P(("gx", "gy"), None, None),
            P(("gx", "gy"), None),
            P(("gx", "gy")),
            P(("gx", "gy")),
            P(("gx", "gy"), None),
        ),
        out_specs=(P(("gx", "gy"), None), P(("gx", "gy"), None, None)),
        check_vma=False,
    )
```

```python
import functools
import math

import jax
import jax.numpy as jnp
import ml_dtypes
import numpy as np
from jax import lax
from jax.experimental import pallas as pl
from jax.experimental.pallas import tpu as pltpu
from jax.sharding import PartitionSpec as P

B = 128
TB = 4
SB = 12
LB = 8
ROWS = 6 * SB
DET = 64
WIN = 256
HALF = 64
EPS = 1e-06
CHUNK = 8
F32 = jnp.float32
BF16 = jnp.bfloat16


def parts(matrix):
    high = matrix.astype(ml_dtypes.bfloat16)
    low = (matrix - high.astype(np.float64)).astype(ml_dtypes.bfloat16)
    return high, low


def tables():
    turns = (np.arange(B)[:, None] * (4 * np.arange(B)[None, :] + 1)) % (4 * B)
    angle = turns * (np.pi / (2 * B))
    forward = np.concatenate(parts(np.concatenate([np.cos(angle), -np.sin(angle)], axis=1)), axis=0)
    back = np.concatenate([np.cos(angle.T), -np.sin(angle.T)], axis=0) / B
    inverse = np.concatenate(parts(back), axis=1)
    n, q = np.arange(B)[:, None], np.arange(B)[None, :]
    ends = np.concatenate([n >= q, n < q], axis=1).astype(ml_dtypes.bfloat16)
    return forward, inverse, np.concatenate([ends, ends], axis=0)


def split(value):
    high = value.astype(BF16)
    return high, (value - high.astype(F32)).astype(BF16)


def dot(a, b):
    return jnp.dot(a, b, preferred_element_type=F32)


def up(value, steps):
    return pltpu.roll(value, value.shape[0] - steps, 0)


def transform(rows, forward):
    out = dot(jnp.concatenate([rows, rows], axis=1), forward)
    return out[:, :B], out[:, B:]


def inverse_dot(real, imag, inverse):
    high, low = split(jnp.concatenate([real, imag], axis=1))
    main = dot(high, inverse)
    return main[:, :B] + main[:, B:] + dot(low, inverse[:, :B])


def ring_layout(ngx, ngy):
    nx = math.isqrt(ngx)
    return {"y": ngx // nx, "x": nx, "z": ngy // 2, "core": 2}


ORDERS = (("x", "y", "z"), ("y", "z", "x"), ("z", "x", "y"))


def kernel(sizes, st, stations, times, partner, wave_in, station_in, time_in, tiles_in, fwd_in, inv_in, ends_in, stack, diff,
           data, near_data, wave, tiles, fwd, inv, ends, rows, station_row, time_row, mine, words, packed,
           xr, xi, wb, rw, pb, sb, xf, pw, lw, lr, li, lq, pq, er, ei, gr, gi,
           send_sem, recv_sem, near_sem, word_sem, load_sem):
    ngx, ngy = sizes
    dims = ring_layout(ngx, ngy)
    groups = ngx * ngy
    gx, gy = lax.axis_index("gx"), lax.axis_index("gy")
    here = {"y": gx // dims["x"], "x": gx % dims["x"], "z": gy // 2, "core": gy % 2}
    mesh_id = pl.DeviceIdType.MESH
    third = 2 * SB

    def device(coords):
        return (coords["y"] * dims["x"] + coords["x"], coords["z"] * 2 + coords["core"])

    def linear(coords):
        return ((coords["y"] * dims["x"] + coords["x"]) * dims["z"] + coords["z"]) * 2 + coords["core"]

    def moved(axis, steps):
        return {**here, axis: (here[axis] + steps + dims[axis]) % dims[axis]}

    loads = []
    for i, (source, target) in enumerate(
        ((wave_in, wave), (station_in, station_row), (time_in, time_row), (fwd_in, fwd), (tiles_in, tiles),
         (inv_in, inv), (ends_in, ends))
    ):
        copy = pltpu.make_async_copy(source, target, load_sem.at[i])
        copy.start()
        loads.append(copy)

    near = (
        ((gx + 1) % ngx, gy),
        ((gx + ngx - 1) % ngx, gy),
        (gx, (gy + 1) % ngy),
        (gx, (gy + ngy - 1) % ngy),
    )
    sibling = device(moved("core", 1))
    peers = [device(moved(axis, r)) for axis in ("x", "y", "z") for r in range(1, dims[axis])]
    peers = peers + [sibling] + list(near)
    barrier = pltpu.get_barrier_semaphore()
    for peer in peers:
        pl.semaphore_signal(barrier, inc=1, device_id=peer, device_id_type=mesh_id)

    loads[0].wait()
    for c in range(3):
        value = wave[c].astype(F32)
        for b in range(SB):
            rows[c, pl.ds(b, 2, stride=SB), :] = value[:, b * B : (b + 1) * B]
        data[here["y"], here["x"], here["z"], here["core"], c] = rows[c].astype(BF16)
    loads[1].wait()
    loads[2].wait()
    mine[...] = jnp.zeros_like(mine)
    mine[:, 0:DET] = station_row[...] * 2048 + time_row[...]
    pl.semaphore_wait(barrier, len(peers))

    def send(source, target, to, send_at, recv_at):
        return pltpu.make_async_remote_copy(
            src_ref=source, dst_ref=target, send_sem=send_at, recv_sem=recv_at, device_id=to, device_id_type=mesh_id)

    def place(coords, whole):
        return tuple(slice(None) if axis in whole else coords[axis] for axis in ("y", "x", "z", "core"))

    def block_copy(coords, whole, c, to, index):
        ref = data.at[place(coords, whole) + (c,)]
        return send(ref, ref, to, send_sem.at[c, index], recv_sem.at[c, index])

    def phase_copy(c, phase, r):
        order = ORDERS[c]
        return block_copy(here, order[:phase], c, device(moved(order[phase], r)), 3 * phase + r - 1)

    def steps(c, phase):
        count = dims[ORDERS[c][phase]]
        return [r for r in (1, 3, 2) if r < count]

    def start_phase(phase):
        for c in range(3):
            if phase:
                for r in steps(c, phase - 1):
                    phase_copy(c, phase - 1, r).wait_recv()
            for r in steps(c, phase):
                phase_copy(c, phase, r).start()

    def plane_copy(c, r):
        return block_copy(moved(ORDERS[c][2], -r), ORDERS[c][:2], c, sibling, 9 + r)

    start_phase(0)
    own_block = data.at[place(here, ()) + (slice(None),)]
    near_copies = []
    for d in range(4):
        near_copies.append(send(mine, words.at[d ^ 1], near[d], word_sem.at[0, d], word_sem.at[1, d ^ 1]))
        near_copies.append(send(own_block, near_data.at[d ^ 1], near[d], near_sem.at[0, d], near_sem.at[1, d ^ 1]))
    for copy in near_copies:
        copy.start()

    for copy in loads[3:]:
        copy.wait()
    forward = fwd[...]
    count = tiles.shape[0]
    square = jnp.zeros((count, B), F32)
    for b in range(3 * TB):
        t = tiles[:, b * B : (b + 1) * B].astype(F32)
        square = square + t * t
    mean = jnp.sum(square, axis=1, keepdims=True) * (1.0 / (3 * TB * B))
    scale = lax.rsqrt((3 * TB * B) * (mean + EPS))
    for b in range(3 * TB):
        real, imag = transform(tiles[:, b * B : (b + 1) * B], forward)
        wb[2 * b] = real * scale
        wb[2 * b + 1] = imag * scale

    start_phase(1)

    moves = ((1, 0), (-1, 0), (0, 1), (0, -1))
    span = 2 * SB
    xf[...] = jnp.zeros_like(xf)
    flat = xf.reshape(8 * xf.shape[0], B)
    valid = []
    for copy in near_copies:
        copy.wait_recv()
    to_scalars = pltpu.make_async_copy(words, packed, load_sem.at[7])
    to_scalars.start()
    for d, (dx, dy) in enumerate(moves + ((0, 0),)):
        nx, ny = gx + dx, gy + dy
        inside = (nx >= 0) & (nx < ngx) & (ny >= 0) & (ny < ngy)
        valid.append(jnp.where(inside, 1.0, 0.0).astype(F32))
        x = (near_data[d] if d < 4 else data[place(here, ())]).astype(F32)
        for c in range(3):
            flat[pl.ds((1 + d * span) * 8 + c, span, stride=8), :] = x[c]
            flat[pl.ds(d * span * 8 + 4 + c, span, stride=8), :] = x[c]
    to_scalars.wait()
    lane = lax.broadcasted_iota(jnp.int32, (8, B), 1)
    upper = lax.broadcasted_iota(jnp.int32, (8, B), 0) < 4
    mask_first = jnp.where(upper & (lane < HALF), 0.0, 1.0).astype(F32)
    mask_last = jnp.where(upper | (lane >= HALF), 0.0, 1.0).astype(F32)

    def window(which, station, start, blocks):
        block, offset = lax.shift_right_logical(start, 7), lax.bitwise_and(start, B - 1)
        base = 1 + which * span + station * SB + block
        shift = lax.bitwise_and(B - offset, B - 1)
        inner = lane < B - offset
        turned = [pltpu.roll(xf[base + j], shift, 1) for j in range(blocks)]
        return [jnp.where(inner, turned[j], turned[j + 1]) for j in range(blocks - 1)]

    def cut_step(e, carry):
        at = pl.ds(pl.multiple_of(e * 8, 8), 8)
        (first,) = window(4, stations[e], times[e], 2)
        lw[at, :] = first
        lq[at, :] = first * first
        for d in range(4):
            word = packed[d, 0, partner[d, e]]
            start = jnp.maximum(lax.bitwise_and(word, 2047) - HALF, 0)
            first, second = window(d, lax.shift_right_logical(word, 11), start, 3)
            pw[d, pl.ds(pl.multiple_of(e * 12, 4), 8), :] = first
            pw[d, pl.ds(pl.multiple_of(e * 12 + 4, 4), 8), :] = second
            pq[d, at, :] = first * first * mask_first + second * second * mask_last
        return carry

    lax.fori_loop(0, DET, cut_step, 0, unroll=4)

    start_phase(2)
    for c in range(3):
        plane_copy(c, 0).start()

    lr[...], li[...] = transform(lw[...].astype(BF16), forward)
    for d in range(4):
        er[d], ei[d] = transform(pw[d].astype(BF16), forward)

    def pair_step(e, carry):
        at = pl.ds(pl.multiple_of(e * 8, 8), 8)
        low, high = pl.ds(pl.multiple_of(e * 12, 4), 8), pl.ds(pl.multiple_of(e * 12 + 4, 4), 8)
        w_re, w_im = lr[at, :], li[at, :]
        for d in range(4):
            x_re = er[d, low, :] + ei[d, high, :]
            x_im = ei[d, low, :] - er[d, high, :]
            gr[d, at, :] = x_re * w_re + x_im * w_im
            gi[d, at, :] = x_im * w_re - x_re * w_im
        return carry

    lax.fori_loop(0, DET, pair_step, 0, unroll=2)

    def gathered(ref, *lead):
        out = ref[lead + (pl.ds(0, DET, stride=8),)]
        for r in range(1, 8):
            out = out + ref[lead + (pl.ds(r, DET, stride=8),)]
        return out

    def mean_of(ref, *lead):
        return jnp.sum(gathered(ref, *lead), axis=1, keepdims=True) * (1.0 / (3 * WIN))

    local_scale = lax.rsqrt((3 * WIN) * (mean_of(lq) + EPS))
    for d in range(4):
        raw = inverse_dot(gathered(gr, d), gathered(gi, d), inv[...])
        scale = local_scale * lax.rsqrt(mean_of(pq, d) + EPS) * valid[d]
        diff[pl.ds(d, DET, stride=4), :] = raw * scale

    def transform_plane(c, coords):
        order = ORDERS[c]
        inner = [axis for axis in ("y", "x", "z") if axis in order[:2]]
        size = dims[inner[0]] * dims[inner[1]]
        x = data[place(coords, order[:2]) + (c,)].astype(F32).reshape(size * third, B)
        real, imag = transform(x.astype(BF16), forward)
        w_re, w_im = real + up(imag, 1), imag - up(real, 1)
        for i in range(size):
            full = {**coords, inner[0]: i // dims[inner[1]], inner[1]: i % dims[inner[1]]}
            for sta in range(2):
                at = 2 * (c * groups + linear(full)) + sta
                begin = i * third + sta * SB
                xr[at, 0:SB] = w_re[begin : begin + SB]
                xi[at, 0:SB] = w_im[begin : begin + SB]

    def energy(core):
        def step(y, carry):
            size = dims["x"] * dims["z"]
            x = data[y, :, :, core].astype(F32)
            sq = x * x
            total = (sq[:, :, 0] + sq[:, :, 1] + sq[:, :, 2]).reshape(size * third, B)
            high, low = split(total)
            sums = dot(jnp.concatenate([high, low], axis=1), ends[...])
            one = sums[:, :B] + up(sums[:, B:], 1)
            two = one + up(one, 1)
            four = two + up(two, 2)
            out = lax.rsqrt(four * (1.0 / (3 * TB * B)) + EPS)
            for i in range(size):
                full = {"y": y, "x": i // dims["z"], "z": i % dims["z"], "core": core}
                for sta in range(2):
                    begin = i * third + sta * SB
                    rw[2 * linear(full) + sta] = out[begin : begin + LB]
            return carry

        lax.fori_loop(0, dims["y"], step, 0)

    side = dims["z"]

    def turn(o):
        return o + (o // 2) * (1 - 2 * (o % 2))

    def own_step(o, carry):
        r = turn(o)
        for c in range(3):
            @pl.when(o > 0)
            def _():
                block_copy(here, ORDERS[c][:2], c, device(moved(ORDERS[c][2], r)), 5 + r).wait_recv()
                plane_copy(c, r).start()
        for c in range(3):
            transform_plane(c, moved(ORDERS[c][2], -r))
        return carry

    lax.fori_loop(0, side, own_step, 0)
    energy(here["core"])

    def other_step(o, carry):
        r = turn(o)
        for c in range(3):
            plane_copy(c, r).wait_recv()
        for c in range(3):
            transform_plane(c, {**moved(ORDERS[c][2], -r), "core": 1 - here["core"]})
        return carry

    lax.fori_loop(0, side, other_step, 0)
    energy(1 - here["core"])

    slots, templates = st.shape

    def product_step(i, carry):
        for k in range(slots):
            s = st[k, i]
            row = i * slots + k
            real = jnp.zeros((LB, B), F32)
            imag = jnp.zeros((LB, B), F32)
            for c in range(3):
                at = s + 2 * c * groups
                for a in range(TB):
                    x_re, x_im = xr[at, a : a + LB], xi[at, a : a + LB]
                    w_re = wb[2 * (c * TB + a), pl.ds(row, 1), :]
                    w_im = wb[2 * (c * TB + a) + 1, pl.ds(row, 1), :]
                    real = real + x_re * w_re + x_im * w_im
                    imag = imag + x_im * w_re - x_re * w_im
            at = pl.ds(pl.multiple_of(row * LB, LB), LB)
            pb[at, :B] = real
            pb[at, B:] = imag
        return carry

    lax.fori_loop(0, templates, product_step, 0)
    group = 2

    def back_step(i, carry):
        size = group * slots * LB
        part = pb[pl.ds(pl.multiple_of(i * size, size), size), :]
        z = inverse_dot(part[:, :B], part[:, B:], inv[...])
        for j in range(group):
            total = jnp.zeros((LB, B), F32)
            for k in range(slots):
                s = st[k, i * group + j]
                row = (j * slots + k) * LB
                total = total + z[row : row + LB] * rw[s]
            sb[pl.ds(pl.multiple_of((i * group + j) * LB, LB), LB), :] = total * (1.0 / math.sqrt(slots))
        return carry

    lax.fori_loop(0, templates // group, back_step, 0, unroll=2)
    for p in range(LB):
        stack[:, p * B : (p + 1) * B] = sb[pl.ds(p, templates, stride=LB), :]

    for copy in near_copies:
        copy.wait_send()
    for c in range(3):
        for phase in range(3):
            for r in steps(c, phase):
                phase_copy(c, phase, r).wait_send()
        for r in range(side):
            plane_copy(c, r).wait_send()


def on_device(waveforms, templates, tpl_stations, det_station, det_time, partner):
    ngx, ngy = lax.axis_size("gx"), lax.axis_size("gy")
    groups = ngx * ngy
    count = templates.shape[0] * templates.shape[1]
    forward, inverse, ends = tables()
    smem = pl.BlockSpec(memory_space=pltpu.SMEM)
    vmem = pl.BlockSpec(memory_space=pltpu.VMEM)
    anywhere = pl.BlockSpec(memory_space=pl.ANY)
    dims = ring_layout(ngx, ngy)
    ntpl = templates.shape[0]

    def floats(*shape):
        return pltpu.VMEM(shape, F32)

    def halves(*shape):
        return pltpu.VMEM(shape, BF16)

    def ints(*shape):
        return pltpu.VMEM(shape, jnp.int32)

    stack, diff = pl.pallas_call(
        functools.partial(kernel, (ngx, ngy)),
        out_shape=(
            jax.ShapeDtypeStruct((ntpl, LB * B), F32),
            jax.ShapeDtypeStruct((4 * DET, B), F32),
        ),
        in_specs=[smem] * 4 + [anywhere] * 7,
        out_specs=(vmem, vmem),
        scratch_shapes=[
            halves(dims["y"], dims["x"], dims["z"], 2, 3, 2 * SB, B),
            halves(4, 3, 2 * SB, B),
            halves(3, 2, SB * B),
            halves(count, 3 * TB * B),
            halves(2 * B, 2 * B),
            halves(2 * B, 2 * B),
            halves(2 * B, 2 * B),
            floats(3, 2 * SB, B),
            ints(1, DET),
            ints(1, DET),
            ints(1, B),
            ints(4, 1, B),
            pltpu.SMEM((4, 1, B), jnp.int32),
            floats(groups * 6, 16, B),
            floats(groups * 6, 16, B),
            floats(6 * TB, count, B),
            floats(groups * 2, LB, B),
            floats(count * LB, 2 * B),
            floats(ntpl * LB, B),
            floats(10 * SB + 4, 8, B),
            floats(4, 12 * DET, B),
            floats(8 * DET, B),
            floats(8 * DET, B),
            floats(8 * DET, B),
            floats(8 * DET, B),
            floats(4, 8 * DET, B),
            floats(4, 12 * DET, B),
            floats(4, 12 * DET, B),
            floats(4, 8 * DET, B),
            floats(4, 8 * DET, B),
            pltpu.SemaphoreType.DMA((3, 13)),
            pltpu.SemaphoreType.DMA((3, 13)),
            pltpu.SemaphoreType.DMA((2, 4)),
            pltpu.SemaphoreType.DMA((2, 4)),
            pltpu.SemaphoreType.DMA((8,)),
        ],
        compiler_params=pltpu.CompilerParams(
            collective_id=0, has_side_effects=True, vmem_limit_bytes=60 * 1024 * 1024
        ),
    )(tpl_stations.T, det_station, det_time, partner.T, jnp.transpose(waveforms, (1, 0, 2)),
      det_station.reshape(1, DET), det_time.reshape(1, DET), templates.reshape(count, 3 * TB * B),
      jnp.asarray(forward), jnp.asarray(inverse), jnp.asarray(ends))
    return stack, diff.reshape(DET, 4, B)


def solution(mesh):
    return jax.shard_map(
        on_device,
        mesh=mesh,
        in_specs=(
            P(("gx", "gy"), None, None),
            P(("gx", "gy"), None, None),
            P(("gx", "gy"), None),
            P(("gx", "gy")),
            P(("gx", "gy")),
            P(("gx", "gy"), None),
        ),
        out_specs=(P(("gx", "gy"), None), P(("gx", "gy"), None, None)),
        check_vma=False,
    )
```

```python
import functools
import math

import jax
import jax.numpy as jnp
import ml_dtypes
import numpy as np
from jax import lax
from jax.experimental import pallas as pl
from jax.experimental.pallas import tpu as pltpu
from jax.sharding import PartitionSpec as P

B = 128
TB = 4
SB = 12
LB = 8
ROWS = 6 * SB
DET = 64
WIN = 256
HALF = 64
EPS = 1e-06
CHUNK = 8
F32 = jnp.float32
BF16 = jnp.bfloat16


def parts(matrix):
    high = matrix.astype(ml_dtypes.bfloat16)
    low = (matrix - high.astype(np.float64)).astype(ml_dtypes.bfloat16)
    return high, low


def tables():
    turns = (np.arange(B)[:, None] * (4 * np.arange(B)[None, :] + 1)) % (4 * B)
    angle = turns * (np.pi / (2 * B))
    forward = np.concatenate(parts(np.concatenate([np.cos(angle), -np.sin(angle)], axis=1)), axis=0)
    back = np.concatenate([np.cos(angle.T), -np.sin(angle.T)], axis=0) / B
    inverse = np.concatenate(parts(back), axis=1)
    n, q = np.arange(B)[:, None], np.arange(B)[None, :]
    ends = np.concatenate([n >= q, n < q], axis=1).astype(ml_dtypes.bfloat16)
    return forward, inverse, np.concatenate([ends, ends], axis=0)


def split(value):
    high = value.astype(BF16)
    return high, (value - high.astype(F32)).astype(BF16)


def dot(a, b):
    return jnp.dot(a, b, preferred_element_type=F32)


def up(value, steps):
    return pltpu.roll(value, value.shape[0] - steps, 0)


def transform(rows, forward):
    out = dot(jnp.concatenate([rows, rows], axis=1), forward)
    return out[:, :B], out[:, B:]


def inverse_dot(real, imag, inverse):
    high, low = split(jnp.concatenate([real, imag], axis=1))
    main = dot(high, inverse)
    return main[:, :B] + main[:, B:] + dot(low, inverse[:, :B])


def ring_layout(ngx, ngy):
    nx = math.isqrt(ngx)
    return {"y": ngx // nx, "x": nx, "z": ngy // 2, "core": 2}


ORDERS = (("x", "y", "z"), ("y", "z", "x"), ("z", "x", "y"))


def kernel(sizes, st_in, stations_in, times_in, partner_in, wave_in, station_in, time_in, tiles_in, fwd_in, inv_in, ends_in, stack, diff,
           data, near_data, wave, tiles, fwd, inv, ends, rows, station_row, time_row, mine, words, packed, st, stations, times, partner,
           xr, xi, wb, rw, pb, sb, xf, pw, lw, lr, li, lq, pq, er, ei, gr, gi,
           send_sem, recv_sem, near_sem, word_sem, load_sem):
    ngx, ngy = sizes
    dims = ring_layout(ngx, ngy)
    groups = ngx * ngy
    gx, gy = lax.axis_index("gx"), lax.axis_index("gy")
    here = {"y": gx // dims["x"], "x": gx % dims["x"], "z": gy // 2, "core": gy % 2}
    mesh_id = pl.DeviceIdType.MESH
    third = 2 * SB

    def device(coords):
        return (coords["y"] * dims["x"] + coords["x"], coords["z"] * 2 + coords["core"])

    def linear(coords):
        return ((coords["y"] * dims["x"] + coords["x"]) * dims["z"] + coords["z"]) * 2 + coords["core"]

    def moved(axis, steps):
        return {**here, axis: (here[axis] + steps + dims[axis]) % dims[axis]}

    loads = []
    for i, (source, target) in enumerate(
        ((wave_in, wave), (station_in, station_row), (time_in, time_row), (fwd_in, fwd), (tiles_in, tiles),
         (inv_in, inv), (ends_in, ends), (st_in, st), (stations_in, stations), (times_in, times), (partner_in, partner))
    ):
        copy = pltpu.make_async_copy(source, target, load_sem.at[i])
        copy.start()
        loads.append(copy)

    near = (
        ((gx + 1) % ngx, gy),
        ((gx + ngx - 1) % ngx, gy),
        (gx, (gy + 1) % ngy),
        (gx, (gy + ngy - 1) % ngy),
    )
    sibling = device(moved("core", 1))
    side = dims["z"]

    def across(c, n):
        first, second = ORDERS[c][:2]
        return {**here, first: (here[first] + n % side) % side, second: (here[second] + n // side) % side}

    barrier = pltpu.get_barrier_semaphore()
    for peer in (sibling,) + near:
        pl.semaphore_signal(barrier, inc=1, device_id=peer, device_id_type=mesh_id)

    def greet(n, carry):
        for c in range(3):
            pl.semaphore_signal(barrier, inc=1, device_id=device(across(c, n)), device_id_type=mesh_id)
        return carry

    lax.fori_loop(1, side * side, greet, 0)

    loads[0].wait()
    for c in range(3):
        value = wave[c].astype(F32)
        for b in range(SB):
            rows[c, pl.ds(b, 2, stride=SB), :] = value[:, b * B : (b + 1) * B]
        data[here["y"], here["x"], here["z"], here["core"], c] = rows[c].astype(BF16)
    loads[1].wait()
    loads[2].wait()
    mine[...] = jnp.zeros_like(mine)
    mine[:, 0:DET] = station_row[...] * 2048 + time_row[...]
    pl.semaphore_wait(barrier, 5 + 3 * (side * side - 1))

    def send(source, target, to, send_at, recv_at):
        return pltpu.make_async_remote_copy(
            src_ref=source, dst_ref=target, send_sem=send_at, recv_sem=recv_at, device_id=to, device_id_type=mesh_id)

    def place(coords, whole):
        return tuple(slice(None) if axis in whole else coords[axis] for axis in ("y", "x", "z", "core"))

    def block_copy(coords, whole, c, to, index):
        ref = data.at[place(coords, whole) + (c,)]
        return send(ref, ref, to, send_sem.at[c, index], recv_sem.at[c, index])

    def own_copy(c, n):
        return block_copy(here, (), c, device(across(c, n)), n - 1)

    def line_copy(c, r):
        return block_copy(here, ORDERS[c][:2], c, device(moved(ORDERS[c][2], r)), 14 + r)

    def each_own(act):
        def step(n, carry):
            for c in range(3):
                act(own_copy(c, n))
            return carry

        lax.fori_loop(1, side * side, step, 0)

    steps = [r for r in (1, 3, 2) if r < side]

    def plane_copy(c, r):
        return block_copy(moved(ORDERS[c][2], -r), ORDERS[c][:2], c, sibling, 18 + r)

    own_block = data.at[place(here, ()) + (slice(None),)]
    near_copies = []
    for d in range(4):
        near_copies.append(send(mine, words.at[d ^ 1], near[d], word_sem.at[0, d], word_sem.at[1, d ^ 1]))
        near_copies.append(send(own_block, near_data.at[d ^ 1], near[d], near_sem.at[0, d], near_sem.at[1, d ^ 1]))
    for copy in near_copies[::2]:
        copy.start()
    each_own(lambda copy: copy.start())
    for copy in near_copies[1::2]:
        copy.start()

    for copy in loads[3:]:
        copy.wait()
    forward = fwd[...]
    count = tiles.shape[0]
    square = jnp.zeros((count, B), F32)
    for b in range(3 * TB):
        t = tiles[:, b * B : (b + 1) * B].astype(F32)
        square = square + t * t
    mean = jnp.sum(square, axis=1, keepdims=True) * (1.0 / (3 * TB * B))
    scale = lax.rsqrt((3 * TB * B) * (mean + EPS))
    for b in range(3 * TB):
        real, imag = transform(tiles[:, b * B : (b + 1) * B], forward)
        wb[2 * b] = real * scale
        wb[2 * b + 1] = imag * scale

    each_own(lambda copy: copy.wait_recv())
    for r in steps:
        for c in range(3):
            line_copy(c, r).start()
    for c in range(3):
        plane_copy(c, 0).start()

    moves = ((1, 0), (-1, 0), (0, 1), (0, -1))
    span = 2 * SB
    xf[...] = jnp.zeros_like(xf)
    flat = xf.reshape(8 * xf.shape[0], B)
    valid = []
    for copy in near_copies:
        copy.wait_recv()
    to_scalars = pltpu.make_async_copy(words, packed, load_sem.at[11])
    to_scalars.start()
    for d, (dx, dy) in enumerate(moves + ((0, 0),)):
        nx, ny = gx + dx, gy + dy
        inside = (nx >= 0) & (nx < ngx) & (ny >= 0) & (ny < ngy)
        valid.append(jnp.where(inside, 1.0, 0.0).astype(F32))
        x = (near_data[d] if d < 4 else data[place(here, ())]).astype(F32)
        for c in range(3):
            flat[pl.ds((1 + d * span) * 8 + c, span, stride=8), :] = x[c]
            flat[pl.ds(d * span * 8 + 4 + c, span, stride=8), :] = x[c]
    to_scalars.wait()
    lane = lax.broadcasted_iota(jnp.int32, (8, B), 1)
    upper = lax.broadcasted_iota(jnp.int32, (8, B), 0) < 4
    mask_first = jnp.where(upper & (lane < HALF), 0.0, 1.0).astype(F32)
    mask_last = jnp.where(upper | (lane >= HALF), 0.0, 1.0).astype(F32)

    def window(which, station, start, blocks):
        block, offset = lax.shift_right_logical(start, 7), lax.bitwise_and(start, B - 1)
        base = 1 + which * span + station * SB + block
        shift = lax.bitwise_and(B - offset, B - 1)
        inner = lane < B - offset
        turned = [pltpu.roll(xf[base + j], shift, 1) for j in range(blocks)]
        return [jnp.where(inner, turned[j], turned[j + 1]) for j in range(blocks - 1)]

    def cut_step(e, carry):
        at = pl.ds(pl.multiple_of(e * 8, 8), 8)
        (first,) = window(4, stations[e], times[e], 2)
        lw[at, :] = first
        lq[at, :] = first * first
        for d in range(4):
            word = packed[d, 0, partner[d, e]]
            start = jnp.maximum(lax.bitwise_and(word, 2047) - HALF, 0)
            first, second = window(d, lax.shift_right_logical(word, 11), start, 3)
            pw[d, pl.ds(pl.multiple_of(e * 12, 4), 8), :] = first
            pw[d, pl.ds(pl.multiple_of(e * 12 + 4, 4), 8), :] = second
            pq[d, at, :] = first * first * mask_first + second * second * mask_last
        return carry

    lax.fori_loop(0, DET, cut_step, 0, unroll=4)

    lr[...], li[...] = transform(lw[...].astype(BF16), forward)
    for d in range(4):
        er[d], ei[d] = transform(pw[d].astype(BF16), forward)

    def pair_step(e, carry):
        at = pl.ds(pl.multiple_of(e * 8, 8), 8)
        low, high = pl.ds(pl.multiple_of(e * 12, 4), 8), pl.ds(pl.multiple_of(e * 12 + 4, 4), 8)
        w_re, w_im = lr[at, :], li[at, :]
        for d in range(4):
            x_re = er[d, low, :] + ei[d, high, :]
            x_im = ei[d, low, :] - er[d, high, :]
            gr[d, at, :] = x_re * w_re + x_im * w_im
            gi[d, at, :] = x_im * w_re - x_re * w_im
        return carry

    lax.fori_loop(0, DET, pair_step, 0, unroll=2)

    def gathered(ref, *lead):
        out = ref[lead + (pl.ds(0, DET, stride=8),)]
        for r in range(1, 8):
            out = out + ref[lead + (pl.ds(r, DET, stride=8),)]
        return out

    def mean_of(ref, *lead):
        return jnp.sum(gathered(ref, *lead), axis=1, keepdims=True) * (1.0 / (3 * WIN))

    local_scale = lax.rsqrt((3 * WIN) * (mean_of(lq) + EPS))
    for d in range(4):
        raw = inverse_dot(gathered(gr, d), gathered(gi, d), inv[...])
        scale = local_scale * lax.rsqrt(mean_of(pq, d) + EPS) * valid[d]
        diff[:, d, :] = raw * scale

    def transform_plane(c, coords):
        order = ORDERS[c]
        inner = [axis for axis in ("y", "x", "z") if axis in order[:2]]
        size = dims[inner[0]] * dims[inner[1]]
        x = data[place(coords, order[:2]) + (c,)].astype(F32).reshape(size * third, B)
        real, imag = transform(x.astype(BF16), forward)
        w_re, w_im = real + up(imag, 1), imag - up(real, 1)
        for i in range(size):
            full = {**coords, inner[0]: i // dims[inner[1]], inner[1]: i % dims[inner[1]]}
            for sta in range(2):
                at = 2 * (c * groups + linear(full)) + sta
                begin = i * third + sta * SB
                xr[at, 0:SB] = w_re[begin : begin + SB]
                xi[at, 0:SB] = w_im[begin : begin + SB]

    def energy(core):
        def step(y, carry):
            size = dims["x"] * dims["z"]
            x = data[y, :, :, core].astype(F32)
            sq = x * x
            total = (sq[:, :, 0] + sq[:, :, 1] + sq[:, :, 2]).reshape(size * third, B)
            high, low = split(total)
            sums = dot(jnp.concatenate([high, low], axis=1), ends[...])
            one = sums[:, :B] + up(sums[:, B:], 1)
            two = one + up(one, 1)
            four = two + up(two, 2)
            out = lax.rsqrt(four * (1.0 / (3 * TB * B)) + EPS)
            for i in range(size):
                full = {"y": y, "x": i // dims["z"], "z": i % dims["z"], "core": core}
                for sta in range(2):
                    begin = i * third + sta * SB
                    rw[2 * linear(full) + sta] = out[begin : begin + LB]
            return carry

        lax.fori_loop(0, dims["y"], step, 0)

    def turn(o):
        return o + (o // 2) * (1 - 2 * (o % 2))

    def own_step(o, carry):
        r = turn(o)
        for c in range(3):
            @pl.when(o > 0)
            def _():
                line_copy(c, r).wait_recv()
                plane_copy(c, r).start()
        for c in range(3):
            transform_plane(c, moved(ORDERS[c][2], -r))
        return carry

    lax.fori_loop(0, side, own_step, 0)
    energy(here["core"])

    def other_step(o, carry):
        r = turn(o)
        for c in range(3):
            plane_copy(c, r).wait_recv()
        for c in range(3):
            transform_plane(c, {**moved(ORDERS[c][2], -r), "core": 1 - here["core"]})
        return carry

    lax.fori_loop(0, side, other_step, 0)
    energy(1 - here["core"])

    slots, templates = st.shape

    def product_step(i, carry):
        for k in range(slots):
            s = st[k, i]
            row = i * slots + k
            real = jnp.zeros((LB, B), F32)
            imag = jnp.zeros((LB, B), F32)
            for c in range(3):
                at = s + 2 * c * groups
                for a in range(TB):
                    x_re, x_im = xr[at, a : a + LB], xi[at, a : a + LB]
                    w_re = wb[2 * (c * TB + a), pl.ds(row, 1), :]
                    w_im = wb[2 * (c * TB + a) + 1, pl.ds(row, 1), :]
                    real = real + x_re * w_re + x_im * w_im
                    imag = imag + x_im * w_re - x_re * w_im
            at = pl.ds(pl.multiple_of(row * LB, LB), LB)
            pb[at, :B] = real
            pb[at, B:] = imag
        return carry

    lax.fori_loop(0, templates, product_step, 0)
    group = 2

    def back_step(i, carry):
        size = group * slots * LB
        part = pb[pl.ds(pl.multiple_of(i * size, size), size), :]
        z = inverse_dot(part[:, :B], part[:, B:], inv[...])
        for j in range(group):
            total = jnp.zeros((LB, B), F32)
            for k in range(slots):
                s = st[k, i * group + j]
                row = (j * slots + k) * LB
                total = total + z[row : row + LB] * rw[s]
            sb[pl.ds(pl.multiple_of((i * group + j) * LB, LB), LB), :] = total * (1.0 / math.sqrt(slots))
        return carry

    lax.fori_loop(0, templates // group, back_step, 0, unroll=2)
    for p in range(LB):
        stack[:, p * B : (p + 1) * B] = sb[pl.ds(p, templates, stride=LB), :]

    for copy in near_copies:
        copy.wait_send()
    each_own(lambda copy: copy.wait_send())
    for c in range(3):
        for r in steps:
            line_copy(c, r).wait_send()
        for r in range(side):
            plane_copy(c, r).wait_send()


def on_device(waveforms, templates, tpl_stations, det_station, det_time, partner):
    ngx, ngy = lax.axis_size("gx"), lax.axis_size("gy")
    groups = ngx * ngy
    count = templates.shape[0] * templates.shape[1]
    forward, inverse, ends = tables()
    vmem = pl.BlockSpec(memory_space=pltpu.VMEM)
    hbm = pl.BlockSpec(memory_space=pltpu.HBM)
    dims = ring_layout(ngx, ngy)
    ntpl, slots = templates.shape[:2]

    def floats(*shape):
        return pltpu.VMEM(shape, F32)

    def halves(*shape):
        return pltpu.VMEM(shape, BF16)

    def ints(*shape):
        return pltpu.VMEM(shape, jnp.int32)

    stack, diff = pl.pallas_call(
        functools.partial(kernel, (ngx, ngy)),
        out_shape=(
            jax.ShapeDtypeStruct((ntpl, LB * B), F32),
            jax.ShapeDtypeStruct((DET, 4, B), F32),
        ),
        in_specs=[hbm] * 11,
        out_specs=(vmem, vmem),
        scratch_shapes=[
            halves(dims["y"], dims["x"], dims["z"], 2, 3, 2 * SB, B),
            halves(4, 3, 2 * SB, B),
            halves(3, 2, SB * B),
            halves(count, 3 * TB * B),
            halves(2 * B, 2 * B),
            halves(2 * B, 2 * B),
            halves(2 * B, 2 * B),
            floats(3, 2 * SB, B),
            ints(1, DET),
            ints(1, DET),
            ints(1, B),
            ints(4, 1, B),
            pltpu.SMEM((4, 1, B), jnp.int32),
            pltpu.SMEM((slots, ntpl), jnp.int32),
            pltpu.SMEM((DET,), jnp.int32),
            pltpu.SMEM((DET,), jnp.int32),
            pltpu.SMEM((4, DET), jnp.int32),
            floats(groups * 6, 16, B),
            floats(groups * 6, 16, B),
            floats(6 * TB, count, B),
            floats(groups * 2, LB, B),
            floats(count * LB, 2 * B),
            floats(ntpl * LB, B),
            floats(10 * SB + 4, 8, B),
            floats(4, 12 * DET, B),
            floats(8 * DET, B),
            floats(8 * DET, B),
            floats(8 * DET, B),
            floats(8 * DET, B),
            floats(4, 8 * DET, B),
            floats(4, 12 * DET, B),
            floats(4, 12 * DET, B),
            floats(4, 8 * DET, B),
            floats(4, 8 * DET, B),
            pltpu.SemaphoreType.DMA((3, 22)),
            pltpu.SemaphoreType.DMA((3, 22)),
            pltpu.SemaphoreType.DMA((2, 4)),
            pltpu.SemaphoreType.DMA((2, 4)),
            pltpu.SemaphoreType.DMA((12,)),
        ],
        compiler_params=pltpu.CompilerParams(
            collective_id=0, has_side_effects=True, vmem_limit_bytes=59 * 1024 * 1024
        ),
    )(tpl_stations.T, det_station, det_time, partner.T, jnp.transpose(waveforms, (1, 0, 2)),
      det_station.reshape(1, DET), det_time.reshape(1, DET), templates.reshape(count, 3 * TB * B),
      jnp.asarray(forward), jnp.asarray(inverse), jnp.asarray(ends))
    return stack, diff


def solution(mesh):
    return jax.shard_map(
        on_device,
        mesh=mesh,
        in_specs=(
            P(("gx", "gy"), None, None),
            P(("gx", "gy"), None, None),
            P(("gx", "gy"), None),
            P(("gx", "gy")),
            P(("gx", "gy")),
            P(("gx", "gy"), None),
        ),
        out_specs=(P(("gx", "gy"), None), P(("gx", "gy"), None, None)),
        check_vma=False,
    )
```

```python
import functools
import math

import jax
import jax.numpy as jnp
import ml_dtypes
import numpy as np
from jax import lax
from jax.experimental import pallas as pl
from jax.experimental.pallas import tpu as pltpu
from jax.sharding import PartitionSpec as P

B = 128
TB = 4
SB = 12
LB = 8
ROWS = 6 * SB
DET = 64
WIN = 256
HALF = 64
EPS = 1e-06
CHUNK = 8
F32 = jnp.float32
BF16 = jnp.bfloat16


def parts(matrix):
    high = matrix.astype(ml_dtypes.bfloat16)
    low = (matrix - high.astype(np.float64)).astype(ml_dtypes.bfloat16)
    return high, low


def tables():
    turns = (np.arange(B)[:, None] * (4 * np.arange(B)[None, :] + 1)) % (4 * B)
    angle = turns * (np.pi / (2 * B))
    forward = np.concatenate(parts(np.concatenate([np.cos(angle), -np.sin(angle)], axis=1)), axis=0)
    back = np.concatenate([np.cos(angle.T), -np.sin(angle.T)], axis=0) / B
    inverse = np.concatenate(parts(back), axis=1)
    n, q = np.arange(B)[:, None], np.arange(B)[None, :]
    ends = np.concatenate([n >= q, n < q], axis=1).astype(ml_dtypes.bfloat16)
    return forward, inverse, np.concatenate([ends, ends], axis=0)


def split(value):
    high = value.astype(BF16)
    return high, (value - high.astype(F32)).astype(BF16)


def dot(a, b):
    return jnp.dot(a, b, preferred_element_type=F32)


def up(value, steps):
    return pltpu.roll(value, value.shape[0] - steps, 0)


def transform(rows, forward):
    out = dot(jnp.concatenate([rows, rows], axis=1), forward)
    return out[:, :B], out[:, B:]


def inverse_dot(real, imag, inverse):
    high, low = split(jnp.concatenate([real, imag], axis=1))
    main = dot(high, inverse)
    return main[:, :B] + main[:, B:] + dot(low, inverse[:, :B])


def ring_layout(ngx, ngy):
    nx = math.isqrt(ngx)
    return {"y": ngx // nx, "x": nx, "z": ngy // 2, "core": 2}


ORDERS = (("x", "y", "z"), ("y", "z", "x"), ("z", "x", "y"))


def kernel(sizes, st_in, stations_in, times_in, partner_in, wave_in, station_in, time_in, tiles_in, fwd_in, inv_in, ends_in, stack, diff,
           data, near_data, wave, tiles, fwd, inv, ends, rows, station_row, time_row, mine, words, packed, st, stations, times, partner,
           xr, xi, wb, rw, pb, sb, xf, pw, lw, lr, li, lq, pq, er, ei, gr, gi,
           send_sem, recv_sem, near_sem, word_sem, load_sem):
    ngx, ngy = sizes
    dims = ring_layout(ngx, ngy)
    groups = ngx * ngy
    gx, gy = lax.axis_index("gx"), lax.axis_index("gy")
    here = {"y": gx // dims["x"], "x": gx % dims["x"], "z": gy // 2, "core": gy % 2}
    mesh_id = pl.DeviceIdType.MESH
    third = 2 * SB

    def device(coords):
        return (coords["y"] * dims["x"] + coords["x"], coords["z"] * 2 + coords["core"])

    def linear(coords):
        return ((coords["y"] * dims["x"] + coords["x"]) * dims["z"] + coords["z"]) * 2 + coords["core"]

    def moved(axis, steps):
        return {**here, axis: (here[axis] + steps + dims[axis]) % dims[axis]}

    loads = []
    for i, (source, target) in enumerate(
        ((wave_in, wave), (station_in, station_row), (time_in, time_row), (fwd_in, fwd), (tiles_in, tiles),
         (inv_in, inv), (ends_in, ends), (st_in, st), (stations_in, stations), (times_in, times), (partner_in, partner))
    ):
        copy = pltpu.make_async_copy(source, target, load_sem.at[i])
        copy.start()
        loads.append(copy)

    near = (
        ((gx + 1) % ngx, gy),
        ((gx + ngx - 1) % ngx, gy),
        (gx, (gy + 1) % ngy),
        (gx, (gy + ngy - 1) % ngy),
    )
    sibling = device(moved("core", 1))
    side = dims["z"]

    def across(c, n):
        first, second = ORDERS[c][:2]
        return {**here, first: (here[first] + n % side) % side, second: (here[second] + n // side) % side}

    barrier = pltpu.get_barrier_semaphore()
    for peer in (sibling,) + near:
        pl.semaphore_signal(barrier, inc=1, device_id=peer, device_id_type=mesh_id)

    def greet(n, carry):
        for c in range(3):
            pl.semaphore_signal(barrier, inc=1, device_id=device(across(c, n)), device_id_type=mesh_id)
        return carry

    lax.fori_loop(1, side * side, greet, 0)

    loads[0].wait()
    for c in range(3):
        value = wave[c].astype(F32)
        for b in range(SB):
            rows[c, pl.ds(b, 2, stride=SB), :] = value[:, b * B : (b + 1) * B]
        data[here["y"], here["x"], here["z"], here["core"], c] = rows[c].astype(BF16)
    loads[1].wait()
    loads[2].wait()
    mine[...] = jnp.zeros_like(mine)
    mine[:, 0:DET] = station_row[...] * 2048 + time_row[...]
    pl.semaphore_wait(barrier, 5 + 3 * (side * side - 1))

    def send(source, target, to, send_at, recv_at):
        return pltpu.make_async_remote_copy(
            src_ref=source, dst_ref=target, send_sem=send_at, recv_sem=recv_at, device_id=to, device_id_type=mesh_id)

    def place(coords, whole):
        return tuple(slice(None) if axis in whole else coords[axis] for axis in ("y", "x", "z", "core"))

    def block_copy(coords, whole, c, to, index):
        ref = data.at[place(coords, whole) + (c,)]
        return send(ref, ref, to, send_sem.at[c, index], recv_sem.at[c, index])

    def own_copy(c, n):
        return block_copy(here, (), c, device(across(c, n)), n - 1)

    def line_copy(c, r):
        return block_copy(here, ORDERS[c][:2], c, device(moved(ORDERS[c][2], r)), 14 + r)

    def each_own(act):
        def step(n, carry):
            for c in range(3):
                act(own_copy(c, n))
            return carry

        lax.fori_loop(1, side * side, step, 0)

    steps = [r for r in (1, 3, 2) if r < side]

    def plane_copy(c, r):
        return block_copy(moved(ORDERS[c][2], -r), ORDERS[c][:2], c, sibling, 18 + r)

    own_block = data.at[place(here, ()) + (slice(None),)]
    near_copies = []
    for d in range(4):
        near_copies.append(send(mine, words.at[d ^ 1], near[d], word_sem.at[0, d], word_sem.at[1, d ^ 1]))
        near_copies.append(send(own_block, near_data.at[d ^ 1], near[d], near_sem.at[0, d], near_sem.at[1, d ^ 1]))
    for copy in near_copies[::2]:
        copy.start()
    each_own(lambda copy: copy.start())
    for copy in near_copies[1::2]:
        copy.start()

    for copy in loads[3:]:
        copy.wait()
    forward = fwd[...]
    count = tiles.shape[0]
    square = jnp.zeros((count, B), F32)
    for b in range(3 * TB):
        t = tiles[:, b * B : (b + 1) * B].astype(F32)
        square = square + t * t
    mean = jnp.sum(square, axis=1, keepdims=True) * (1.0 / (3 * TB * B))
    scale = lax.rsqrt((3 * TB * B) * (mean + EPS))
    for b in range(3 * TB):
        real, imag = transform(tiles[:, b * B : (b + 1) * B], forward)
        wb[2 * b] = real * scale
        wb[2 * b + 1] = imag * scale

    each_own(lambda copy: copy.wait_recv())
    for r in steps:
        for c in range(3):
            line_copy(c, r).start()
    for c in range(3):
        plane_copy(c, 0).start()

    moves = ((1, 0), (-1, 0), (0, 1), (0, -1))
    span = 2 * SB
    xf[...] = jnp.zeros_like(xf)
    flat = xf.reshape(8 * xf.shape[0], B)
    valid = []
    for copy in near_copies:
        copy.wait_recv()
    to_scalars = pltpu.make_async_copy(words, packed, load_sem.at[11])
    to_scalars.start()
    for d, (dx, dy) in enumerate(moves + ((0, 0),)):
        nx, ny = gx + dx, gy + dy
        inside = (nx >= 0) & (nx < ngx) & (ny >= 0) & (ny < ngy)
        valid.append(jnp.where(inside, 1.0, 0.0).astype(F32))
        x = (near_data[d] if d < 4 else data[place(here, ())]).astype(F32)
        for c in range(3):
            flat[pl.ds((1 + d * span) * 8 + c, span, stride=8), :] = x[c]
            flat[pl.ds(d * span * 8 + 4 + c, span, stride=8), :] = x[c]
    to_scalars.wait()
    lane = lax.broadcasted_iota(jnp.int32, (8, B), 1)
    upper = lax.broadcasted_iota(jnp.int32, (8, B), 0) < 4
    mask_first = jnp.where(upper & (lane < HALF), 0.0, 1.0).astype(F32)
    mask_last = jnp.where(upper | (lane >= HALF), 0.0, 1.0).astype(F32)

    def window(which, station, start, blocks):
        block, offset = lax.shift_right_logical(start, 7), lax.bitwise_and(start, B - 1)
        base = 1 + which * span + station * SB + block
        shift = lax.bitwise_and(B - offset, B - 1)
        inner = lane < B - offset
        turned = [pltpu.roll(xf[base + j], shift, 1) for j in range(blocks)]
        return [jnp.where(inner, turned[j], turned[j + 1]) for j in range(blocks - 1)]

    def cut_step(e, carry):
        at = pl.ds(pl.multiple_of(e * 8, 8), 8)
        (first,) = window(4, stations[e], times[e], 2)
        lw[at, :] = first
        lq[at, :] = first * first
        for d in range(4):
            word = packed[d, 0, partner[d, e]]
            start = jnp.maximum(lax.bitwise_and(word, 2047) - HALF, 0)
            first, second = window(d, lax.shift_right_logical(word, 11), start, 3)
            pw[d, pl.ds(pl.multiple_of(e * 12, 4), 8), :] = first
            pw[d, pl.ds(pl.multiple_of(e * 12 + 4, 4), 8), :] = second
            pq[d, at, :] = first * first * mask_first + second * second * mask_last
        return carry

    lax.fori_loop(0, DET, cut_step, 0, unroll=8)

    lr[...], li[...] = transform(lw[...].astype(BF16), forward)
    for d in range(4):
        er[d], ei[d] = transform(pw[d].astype(BF16), forward)

    def pair_step(e, carry):
        at = pl.ds(pl.multiple_of(e * 8, 8), 8)
        low, high = pl.ds(pl.multiple_of(e * 12, 4), 8), pl.ds(pl.multiple_of(e * 12 + 4, 4), 8)
        w_re, w_im = lr[at, :], li[at, :]
        for d in range(4):
            x_re = er[d, low, :] + ei[d, high, :]
            x_im = ei[d, low, :] - er[d, high, :]
            gr[d, at, :] = x_re * w_re + x_im * w_im
            gi[d, at, :] = x_im * w_re - x_re * w_im
        return carry

    lax.fori_loop(0, DET, pair_step, 0, unroll=2)

    def gathered(ref, *lead):
        out = ref[lead + (pl.ds(0, DET, stride=8),)]
        for r in range(1, 8):
            out = out + ref[lead + (pl.ds(r, DET, stride=8),)]
        return out

    def mean_of(ref, *lead):
        return jnp.sum(gathered(ref, *lead), axis=1, keepdims=True) * (1.0 / (3 * WIN))

    local_scale = lax.rsqrt((3 * WIN) * (mean_of(lq) + EPS))
    for d in range(4):
        raw = inverse_dot(gathered(gr, d), gathered(gi, d), inv[...])
        scale = local_scale * lax.rsqrt(mean_of(pq, d) + EPS) * valid[d]
        diff[:, d, :] = raw * scale

    def transform_plane(c, coords):
        order = ORDERS[c]
        inner = [axis for axis in ("y", "x", "z") if axis in order[:2]]
        size = dims[inner[0]] * dims[inner[1]]
        x = data[place(coords, order[:2]) + (c,)].astype(F32).reshape(size * third, B)
        real, imag = transform(x.astype(BF16), forward)
        w_re, w_im = real + up(imag, 1), imag - up(real, 1)
        for i in range(size):
            full = {**coords, inner[0]: i // dims[inner[1]], inner[1]: i % dims[inner[1]]}
            for sta in range(2):
                at = 2 * (c * groups + linear(full)) + sta
                begin = i * third + sta * SB
                xr[at, 0:SB] = w_re[begin : begin + SB]
                xi[at, 0:SB] = w_im[begin : begin + SB]

    def energy(core):
        def step(y, carry):
            size = dims["x"] * dims["z"]
            x = data[y, :, :, core].astype(F32)
            sq = x * x
            total = (sq[:, :, 0] + sq[:, :, 1] + sq[:, :, 2]).reshape(size * third, B)
            high, low = split(total)
            sums = dot(jnp.concatenate([high, low], axis=1), ends[...])
            one = sums[:, :B] + up(sums[:, B:], 1)
            two = one + up(one, 1)
            four = two + up(two, 2)
            out = lax.rsqrt(four * (1.0 / (3 * TB * B)) + EPS)
            for i in range(size):
                full = {"y": y, "x": i // dims["z"], "z": i % dims["z"], "core": core}
                for sta in range(2):
                    begin = i * third + sta * SB
                    rw[2 * linear(full) + sta] = out[begin : begin + LB]
            return carry

        lax.fori_loop(0, dims["y"], step, 0)

    def turn(o):
        return o + (o // 2) * (1 - 2 * (o % 2))

    def own_step(o, carry):
        r = turn(o)
        for c in range(3):
            @pl.when(o > 0)
            def _():
                line_copy(c, r).wait_recv()
                plane_copy(c, r).start()
        for c in range(3):
            transform_plane(c, moved(ORDERS[c][2], -r))
        return carry

    lax.fori_loop(0, side, own_step, 0)
    energy(here["core"])

    def other_step(o, carry):
        r = turn(o)
        for c in range(3):
            plane_copy(c, r).wait_recv()
        for c in range(3):
            transform_plane(c, {**moved(ORDERS[c][2], -r), "core": 1 - here["core"]})
        return carry

    lax.fori_loop(0, side, other_step, 0)
    energy(1 - here["core"])

    slots, templates = st.shape

    def product_step(i, carry):
        for k in range(slots):
            s = st[k, i]
            row = i * slots + k
            real = jnp.zeros((LB, B), F32)
            imag = jnp.zeros((LB, B), F32)
            for c in range(3):
                at = s + 2 * c * groups
                for a in range(TB):
                    x_re, x_im = xr[at, a : a + LB], xi[at, a : a + LB]
                    w_re = wb[2 * (c * TB + a), pl.ds(row, 1), :]
                    w_im = wb[2 * (c * TB + a) + 1, pl.ds(row, 1), :]
                    real = real + x_re * w_re + x_im * w_im
                    imag = imag + x_im * w_re - x_re * w_im
            at = pl.ds(pl.multiple_of(row * LB, LB), LB)
            pb[at, :B] = real
            pb[at, B:] = imag
        return carry

    lax.fori_loop(0, templates, product_step, 0)
    group = 4

    def back_step(i, carry):
        size = group * slots * LB
        part = pb[pl.ds(pl.multiple_of(i * size, size), size), :]
        z = inverse_dot(part[:, :B], part[:, B:], inv[...])
        for j in range(group):
            total = jnp.zeros((LB, B), F32)
            for k in range(slots):
                s = st[k, i * group + j]
                row = (j * slots + k) * LB
                total = total + z[row : row + LB] * rw[s]
            sb[pl.ds(pl.multiple_of((i * group + j) * LB, LB), LB), :] = total * (1.0 / math.sqrt(slots))
        return carry

    lax.fori_loop(0, templates // group, back_step, 0, unroll=2)
    for p in range(LB):
        stack[:, p * B : (p + 1) * B] = sb[pl.ds(p, templates, stride=LB), :]

    for copy in near_copies:
        copy.wait_send()
    each_own(lambda copy: copy.wait_send())
    for c in range(3):
        for r in steps:
            line_copy(c, r).wait_send()
        for r in range(side):
            plane_copy(c, r).wait_send()


def on_device(waveforms, templates, tpl_stations, det_station, det_time, partner):
    ngx, ngy = lax.axis_size("gx"), lax.axis_size("gy")
    groups = ngx * ngy
    count = templates.shape[0] * templates.shape[1]
    forward, inverse, ends = tables()
    vmem = pl.BlockSpec(memory_space=pltpu.VMEM)
    hbm = pl.BlockSpec(memory_space=pltpu.HBM)
    dims = ring_layout(ngx, ngy)
    ntpl, slots = templates.shape[:2]

    def floats(*shape):
        return pltpu.VMEM(shape, F32)

    def halves(*shape):
        return pltpu.VMEM(shape, BF16)

    def ints(*shape):
        return pltpu.VMEM(shape, jnp.int32)

    stack, diff = pl.pallas_call(
        functools.partial(kernel, (ngx, ngy)),
        out_shape=(
            jax.ShapeDtypeStruct((ntpl, LB * B), F32),
            jax.ShapeDtypeStruct((DET, 4, B), F32),
        ),
        in_specs=[hbm] * 11,
        out_specs=(vmem, vmem),
        scratch_shapes=[
            halves(dims["y"], dims["x"], dims["z"], 2, 3, 2 * SB, B),
            halves(4, 3, 2 * SB, B),
            halves(3, 2, SB * B),
            halves(count, 3 * TB * B),
            halves(2 * B, 2 * B),
            halves(2 * B, 2 * B),
            halves(2 * B, 2 * B),
            floats(3, 2 * SB, B),
            ints(1, DET),
            ints(1, DET),
            ints(1, B),
            ints(4, 1, B),
            pltpu.SMEM((4, 1, B), jnp.int32),
            pltpu.SMEM((slots, ntpl), jnp.int32),
            pltpu.SMEM((DET,), jnp.int32),
            pltpu.SMEM((DET,), jnp.int32),
            pltpu.SMEM((4, DET), jnp.int32),
            floats(groups * 6, 16, B),
            floats(groups * 6, 16, B),
            floats(6 * TB, count, B),
            floats(groups * 2, LB, B),
            floats(count * LB, 2 * B),
            floats(ntpl * LB, B),
            floats(10 * SB + 4, 8, B),
            floats(4, 12 * DET, B),
            floats(8 * DET, B),
            floats(8 * DET, B),
            floats(8 * DET, B),
            floats(8 * DET, B),
            floats(4, 8 * DET, B),
            floats(4, 12 * DET, B),
            floats(4, 12 * DET, B),
            floats(4, 8 * DET, B),
            floats(4, 8 * DET, B),
            pltpu.SemaphoreType.DMA((3, 22)),
            pltpu.SemaphoreType.DMA((3, 22)),
            pltpu.SemaphoreType.DMA((2, 4)),
            pltpu.SemaphoreType.DMA((2, 4)),
            pltpu.SemaphoreType.DMA((12,)),
        ],
        compiler_params=pltpu.CompilerParams(
            collective_id=0, has_side_effects=True, vmem_limit_bytes=59 * 1024 * 1024
        ),
    )(tpl_stations.T, det_station, det_time, partner.T, jnp.transpose(waveforms, (1, 0, 2)),
      det_station.reshape(1, DET), det_time.reshape(1, DET), templates.reshape(count, 3 * TB * B),
      jnp.asarray(forward), jnp.asarray(inverse), jnp.asarray(ends))
    return stack, diff


def solution(mesh):
    return jax.shard_map(
        on_device,
        mesh=mesh,
        in_specs=(
            P(("gx", "gy"), None, None),
            P(("gx", "gy"), None, None),
            P(("gx", "gy"), None),
            P(("gx", "gy")),
            P(("gx", "gy")),
            P(("gx", "gy"), None),
        ),
        out_specs=(P(("gx", "gy"), None), P(("gx", "gy"), None, None)),
        check_vma=False,
    )
```

```python
import functools
import math

import jax
import jax.numpy as jnp
import ml_dtypes
import numpy as np
from jax import lax
from jax.experimental import pallas as pl
from jax.experimental.pallas import tpu as pltpu
from jax.sharding import PartitionSpec as P

B = 128
TB = 4
SB = 12
LB = 8
ROWS = 6 * SB
DET = 64
WIN = 256
HALF = 64
EPS = 1e-06
CHUNK = 8
F32 = jnp.float32
BF16 = jnp.bfloat16


def parts(matrix):
    high = matrix.astype(ml_dtypes.bfloat16)
    low = (matrix - high.astype(np.float64)).astype(ml_dtypes.bfloat16)
    return high, low


def tables():
    turns = (np.arange(B)[:, None] * (4 * np.arange(B)[None, :] + 1)) % (4 * B)
    angle = turns * (np.pi / (2 * B))
    forward = np.concatenate(parts(np.concatenate([np.cos(angle), -np.sin(angle)], axis=1)), axis=0)
    back = np.concatenate([np.cos(angle.T), -np.sin(angle.T)], axis=0) / B
    inverse = np.concatenate(parts(back), axis=1)
    n, q = np.arange(B)[:, None], np.arange(B)[None, :]
    ends = np.concatenate([n >= q, n < q], axis=1).astype(ml_dtypes.bfloat16)
    return forward, inverse, np.concatenate([ends, ends], axis=0)


def split(value):
    high = value.astype(BF16)
    return high, (value - high.astype(F32)).astype(BF16)


def dot(a, b):
    return jnp.dot(a, b, preferred_element_type=F32)


def up(value, steps):
    return pltpu.roll(value, value.shape[0] - steps, 0)


def transform(rows, forward):
    out = dot(jnp.concatenate([rows, rows], axis=1), forward)
    return out[:, :B], out[:, B:]


def inverse_dot(real, imag, inverse):
    high, low = split(jnp.concatenate([real, imag], axis=1))
    main = dot(high, inverse)
    return main[:, :B] + main[:, B:] + dot(low, inverse[:, :B])


def ring_layout(ngx, ngy):
    nx = math.isqrt(ngx)
    return {"y": ngx // nx, "x": nx, "z": ngy // 2, "core": 2}


ORDERS = (("x", "y", "z"), ("y", "z", "x"), ("z", "x", "y"))


def kernel(sizes, st_in, stations_in, times_in, partner_in, wave_in, station_in, time_in, tiles_in, fwd_in, inv_in, ends_in, stack, diff,
           data, near_data, wave, tiles, fwd, inv, ends, rows, station_row, time_row, mine, words, packed, st, stations, times, partner,
           xr, xi, wb, rw, pb, sb, xf, pw, lw, lr, li, lq, pq, er, ei, gr, gi,
           send_sem, recv_sem, near_sem, word_sem, load_sem):
    ngx, ngy = sizes
    dims = ring_layout(ngx, ngy)
    groups = ngx * ngy
    gx, gy = lax.axis_index("gx"), lax.axis_index("gy")
    here = {"y": gx // dims["x"], "x": gx % dims["x"], "z": gy // 2, "core": gy % 2}
    mesh_id = pl.DeviceIdType.MESH
    third = 2 * SB

    def device(coords):
        return (coords["y"] * dims["x"] + coords["x"], coords["z"] * 2 + coords["core"])

    def linear(coords):
        return ((coords["y"] * dims["x"] + coords["x"]) * dims["z"] + coords["z"]) * 2 + coords["core"]

    def moved(axis, steps):
        return {**here, axis: (here[axis] + steps + dims[axis]) % dims[axis]}

    loads = []
    for i, (source, target) in enumerate(
        ((wave_in, wave), (station_in, station_row), (time_in, time_row), (fwd_in, fwd), (tiles_in, tiles),
         (inv_in, inv), (ends_in, ends), (st_in, st), (stations_in, stations), (times_in, times), (partner_in, partner))
    ):
        copy = pltpu.make_async_copy(source, target, load_sem.at[i])
        copy.start()
        loads.append(copy)

    near = (
        ((gx + 1) % ngx, gy),
        ((gx + ngx - 1) % ngx, gy),
        (gx, (gy + 1) % ngy),
        (gx, (gy + ngy - 1) % ngy),
    )
    sibling = device(moved("core", 1))
    side = dims["z"]

    def across(c, n):
        first, second = ORDERS[c][:2]
        return {**here, first: (here[first] + n % side) % side, second: (here[second] + n // side) % side}

    barrier = pltpu.get_barrier_semaphore()
    for peer in (sibling,) + near:
        pl.semaphore_signal(barrier, inc=1, device_id=peer, device_id_type=mesh_id)

    def greet(n, carry):
        for c in range(3):
            pl.semaphore_signal(barrier, inc=1, device_id=device(across(c, n)), device_id_type=mesh_id)
        return carry

    lax.fori_loop(1, side * side, greet, 0)

    loads[0].wait()
    for c in range(3):
        value = wave[c].astype(F32)
        for b in range(SB):
            rows[c, pl.ds(b, 2, stride=SB), :] = value[:, b * B : (b + 1) * B]
        data[here["y"], here["x"], here["z"], here["core"], c] = rows[c].astype(BF16)
    loads[1].wait()
    loads[2].wait()
    mine[...] = jnp.zeros_like(mine)
    mine[:, 0:DET] = station_row[...] * 2048 + time_row[...]
    pl.semaphore_wait(barrier, 5 + 3 * (side * side - 1))

    def send(source, target, to, send_at, recv_at):
        return pltpu.make_async_remote_copy(
            src_ref=source, dst_ref=target, send_sem=send_at, recv_sem=recv_at, device_id=to, device_id_type=mesh_id)

    def place(coords, whole):
        return tuple(slice(None) if axis in whole else coords[axis] for axis in ("y", "x", "z", "core"))

    def block_copy(coords, whole, c, to, index):
        ref = data.at[place(coords, whole) + (c,)]
        return send(ref, ref, to, send_sem.at[c, index], recv_sem.at[c, index])

    def own_copy(c, n):
        return block_copy(here, (), c, device(across(c, n)), n - 1)

    def line_copy(c, r):
        return block_copy(here, ORDERS[c][:2], c, device(moved(ORDERS[c][2], r)), 14 + r)

    def each_own(act):
        def step(n, carry):
            for c in range(3):
                act(own_copy(c, n))
            return carry

        lax.fori_loop(1, side * side, step, 0)

    steps = [r for r in (1, 3, 2) if r < side]

    def plane_copy(c, r):
        return block_copy(moved(ORDERS[c][2], -r), ORDERS[c][:2], c, sibling, 18 + r)

    own_block = data.at[place(here, ()) + (slice(None),)]
    near_copies = []
    for d in range(4):
        near_copies.append(send(mine, words.at[d ^ 1], near[d], word_sem.at[0, d], word_sem.at[1, d ^ 1]))
        near_copies.append(send(own_block, near_data.at[d ^ 1], near[d], near_sem.at[0, d], near_sem.at[1, d ^ 1]))
    for copy in near_copies[::2]:
        copy.start()
    each_own(lambda copy: copy.start())
    for copy in near_copies[1::2]:
        copy.start()

    for copy in loads[3:]:
        copy.wait()
    forward = fwd[...]
    count = tiles.shape[0]
    square = jnp.zeros((count, B), F32)
    for b in range(3 * TB):
        t = tiles[:, b * B : (b + 1) * B].astype(F32)
        square = square + t * t
    mean = jnp.sum(square, axis=1, keepdims=True) * (1.0 / (3 * TB * B))
    scale = lax.rsqrt((3 * TB * B) * (mean + EPS))
    for b in range(3 * TB):
        real, imag = transform(tiles[:, b * B : (b + 1) * B], forward)
        wb[2 * b] = real * scale
        wb[2 * b + 1] = imag * scale

    each_own(lambda copy: copy.wait_recv())
    for r in steps:
        for c in range(3):
            line_copy(c, r).start()
    for c in range(3):
        plane_copy(c, 0).start()

    moves = ((1, 0), (-1, 0), (0, 1), (0, -1))
    span = 2 * SB
    xf[...] = jnp.zeros_like(xf)
    flat = xf.reshape(8 * xf.shape[0], B)
    valid = []
    for copy in near_copies:
        copy.wait_recv()
    to_scalars = pltpu.make_async_copy(words, packed, load_sem.at[11])
    to_scalars.start()
    for d, (dx, dy) in enumerate(moves + ((0, 0),)):
        nx, ny = gx + dx, gy + dy
        inside = (nx >= 0) & (nx < ngx) & (ny >= 0) & (ny < ngy)
        valid.append(jnp.where(inside, 1.0, 0.0).astype(F32))
        x = (near_data[d] if d < 4 else data[place(here, ())]).astype(F32)
        for c in range(3):
            flat[pl.ds((1 + d * span) * 8 + c, span, stride=8), :] = x[c]
            flat[pl.ds(d * span * 8 + 4 + c, span, stride=8), :] = x[c]
    to_scalars.wait()
    lane = lax.broadcasted_iota(jnp.int32, (8, B), 1)
    upper = lax.broadcasted_iota(jnp.int32, (8, B), 0) < 4
    mask_first = jnp.where(upper & (lane < HALF), 0.0, 1.0).astype(F32)
    mask_last = jnp.where(upper | (lane >= HALF), 0.0, 1.0).astype(F32)

    def window(which, station, start, blocks):
        block, offset = lax.shift_right_logical(start, 7), lax.bitwise_and(start, B - 1)
        base = 1 + which * span + station * SB + block
        shift = lax.bitwise_and(B - offset, B - 1)
        inner = lane < B - offset
        turned = [pltpu.roll(xf[base + j], shift, 1) for j in range(blocks)]
        return [jnp.where(inner, turned[j], turned[j + 1]) for j in range(blocks - 1)]

    def cut_step(e, carry):
        at = pl.ds(pl.multiple_of(e * 8, 8), 8)
        (first,) = window(4, stations[e], times[e], 2)
        lw[at, :] = first
        lq[at, :] = first * first
        for d in range(4):
            word = packed[d, 0, partner[d, e]]
            start = jnp.maximum(lax.bitwise_and(word, 2047) - HALF, 0)
            first, second = window(d, lax.shift_right_logical(word, 11), start, 3)
            pw[d, pl.ds(pl.multiple_of(e * 12, 4), 8), :] = first
            pw[d, pl.ds(pl.multiple_of(e * 12 + 4, 4), 8), :] = second
            pq[d, at, :] = first * first * mask_first + second * second * mask_last
        return carry

    lax.fori_loop(0, DET, cut_step, 0, unroll=8)

    lr[...], li[...] = transform(lw[...].astype(BF16), forward)
    for d in range(4):
        er[d], ei[d] = transform(pw[d].astype(BF16), forward)

    def pair_step(e, carry):
        at = pl.ds(pl.multiple_of(e * 8, 8), 8)
        low, high = pl.ds(pl.multiple_of(e * 12, 4), 8), pl.ds(pl.multiple_of(e * 12 + 4, 4), 8)
        w_re, w_im = lr[at, :], li[at, :]
        for d in range(4):
            x_re = er[d, low, :] + ei[d, high, :]
            x_im = ei[d, low, :] - er[d, high, :]
            gr[d, at, :] = x_re * w_re + x_im * w_im
            gi[d, at, :] = x_im * w_re - x_re * w_im
        return carry

    lax.fori_loop(0, DET, pair_step, 0, unroll=2)

    def gathered(ref, *lead):
        out = ref[lead + (pl.ds(0, DET, stride=8),)]
        for r in range(1, 8):
            out = out + ref[lead + (pl.ds(r, DET, stride=8),)]
        return out

    def mean_of(ref, *lead):
        return jnp.sum(gathered(ref, *lead), axis=1, keepdims=True) * (1.0 / (3 * WIN))

    local_scale = lax.rsqrt((3 * WIN) * (mean_of(lq) + EPS))
    for d in range(4):
        raw = inverse_dot(gathered(gr, d), gathered(gi, d), inv[...])
        scale = local_scale * lax.rsqrt(mean_of(pq, d) + EPS) * valid[d]
        diff[:, d, :] = raw * scale

    def transform_plane(c, coords):
        order = ORDERS[c]
        inner = [axis for axis in ("y", "x", "z") if axis in order[:2]]
        size = dims[inner[0]] * dims[inner[1]]
        x = data[place(coords, order[:2]) + (c,)].astype(F32).reshape(size * third, B)
        real, imag = transform(x.astype(BF16), forward)
        w_re, w_im = real + up(imag, 1), imag - up(real, 1)
        for i in range(size):
            full = {**coords, inner[0]: i // dims[inner[1]], inner[1]: i % dims[inner[1]]}
            for sta in range(2):
                at = 2 * (c * groups + linear(full)) + sta
                begin = i * third + sta * SB
                xr[at, 0:SB] = w_re[begin : begin + SB]
                xi[at, 0:SB] = w_im[begin : begin + SB]

    def energy(core):
        def step(y, carry):
            size = dims["x"] * dims["z"]
            x = data[y, :, :, core].astype(F32)
            sq = x * x
            total = (sq[:, :, 0] + sq[:, :, 1] + sq[:, :, 2]).reshape(size * third, B)
            high, low = split(total)
            sums = dot(jnp.concatenate([high, low], axis=1), ends[...])
            one = sums[:, :B] + up(sums[:, B:], 1)
            two = one + up(one, 1)
            four = two + up(two, 2)
            out = lax.rsqrt(four * (1.0 / (3 * TB * B)) + EPS)
            for i in range(size):
                full = {"y": y, "x": i // dims["z"], "z": i % dims["z"], "core": core}
                for sta in range(2):
                    begin = i * third + sta * SB
                    rw[2 * linear(full) + sta] = out[begin : begin + LB]
            return carry

        lax.fori_loop(0, dims["y"], step, 0, unroll=2)

    def turn(o):
        return o + (o // 2) * (1 - 2 * (o % 2))

    def own_step(o, carry):
        r = turn(o)
        for c in range(3):
            @pl.when(o > 0)
            def _():
                line_copy(c, r).wait_recv()
                plane_copy(c, r).start()
        for c in range(3):
            transform_plane(c, moved(ORDERS[c][2], -r))
        return carry

    lax.fori_loop(0, side, own_step, 0)
    energy(here["core"])

    def other_step(o, carry):
        r = turn(o)
        for c in range(3):
            plane_copy(c, r).wait_recv()
        for c in range(3):
            transform_plane(c, {**moved(ORDERS[c][2], -r), "core": 1 - here["core"]})
        return carry

    lax.fori_loop(0, side, other_step, 0)
    energy(1 - here["core"])

    slots, templates = st.shape

    def product_step(i, carry):
        for k in range(slots):
            s = st[k, i]
            row = i * slots + k
            real = jnp.zeros((LB, B), F32)
            imag = jnp.zeros((LB, B), F32)
            for c in range(3):
                at = s + 2 * c * groups
                for a in range(TB):
                    x_re, x_im = xr[at, a : a + LB], xi[at, a : a + LB]
                    w_re = wb[2 * (c * TB + a), pl.ds(row, 1), :]
                    w_im = wb[2 * (c * TB + a) + 1, pl.ds(row, 1), :]
                    real = real + x_re * w_re + x_im * w_im
                    imag = imag + x_im * w_re - x_re * w_im
            at = pl.ds(pl.multiple_of(row * LB, LB), LB)
            pb[at, :B] = real
            pb[at, B:] = imag
        return carry

    lax.fori_loop(0, templates, product_step, 0)
    group = 4

    def back_step(i, carry):
        size = group * slots * LB
        part = pb[pl.ds(pl.multiple_of(i * size, size), size), :]
        z = inverse_dot(part[:, :B], part[:, B:], inv[...])
        for j in range(group):
            total = jnp.zeros((LB, B), F32)
            for k in range(slots):
                s = st[k, i * group + j]
                row = (j * slots + k) * LB
                total = total + z[row : row + LB] * rw[s]
            sb[pl.ds(pl.multiple_of((i * group + j) * LB, LB), LB), :] = total * (1.0 / math.sqrt(slots))
        return carry

    lax.fori_loop(0, templates // group, back_step, 0, unroll=2)
    for p in range(LB):
        stack[:, p * B : (p + 1) * B] = sb[pl.ds(p, templates, stride=LB), :]

    for copy in near_copies:
        copy.wait_send()
    each_own(lambda copy: copy.wait_send())
    for c in range(3):
        for r in steps:
            line_copy(c, r).wait_send()
        for r in range(side):
            plane_copy(c, r).wait_send()


def on_device(waveforms, templates, tpl_stations, det_station, det_time, partner):
    ngx, ngy = lax.axis_size("gx"), lax.axis_size("gy")
    groups = ngx * ngy
    count = templates.shape[0] * templates.shape[1]
    forward, inverse, ends = tables()
    vmem = pl.BlockSpec(memory_space=pltpu.VMEM)
    hbm = pl.BlockSpec(memory_space=pltpu.HBM)
    dims = ring_layout(ngx, ngy)
    ntpl, slots = templates.shape[:2]

    def floats(*shape):
        return pltpu.VMEM(shape, F32)

    def halves(*shape):
        return pltpu.VMEM(shape, BF16)

    def ints(*shape):
        return pltpu.VMEM(shape, jnp.int32)

    stack, diff = pl.pallas_call(
        functools.partial(kernel, (ngx, ngy)),
        out_shape=(
            jax.ShapeDtypeStruct((ntpl, LB * B), F32),
            jax.ShapeDtypeStruct((DET, 4, B), F32),
        ),
        in_specs=[hbm] * 11,
        out_specs=(vmem, vmem),
        scratch_shapes=[
            halves(dims["y"], dims["x"], dims["z"], 2, 3, 2 * SB, B),
            halves(4, 3, 2 * SB, B),
            halves(3, 2, SB * B),
            halves(count, 3 * TB * B),
            halves(2 * B, 2 * B),
            halves(2 * B, 2 * B),
            halves(2 * B, 2 * B),
            floats(3, 2 * SB, B),
            ints(1, DET),
            ints(1, DET),
            ints(1, B),
            ints(4, 1, B),
            pltpu.SMEM((4, 1, B), jnp.int32),
            pltpu.SMEM((slots, ntpl), jnp.int32),
            pltpu.SMEM((DET,), jnp.int32),
            pltpu.SMEM((DET,), jnp.int32),
            pltpu.SMEM((4, DET), jnp.int32),
            floats(groups * 6, 16, B),
            floats(groups * 6, 16, B),
            floats(6 * TB, count, B),
            floats(groups * 2, LB, B),
            floats(count * LB, 2 * B),
            floats(ntpl * LB, B),
            floats(10 * SB + 4, 8, B),
            floats(4, 12 * DET, B),
            floats(8 * DET, B),
            floats(8 * DET, B),
            floats(8 * DET, B),
            floats(8 * DET, B),
            floats(4, 8 * DET, B),
            floats(4, 12 * DET, B),
            floats(4, 12 * DET, B),
            floats(4, 8 * DET, B),
            floats(4, 8 * DET, B),
            pltpu.SemaphoreType.DMA((3, 22)),
            pltpu.SemaphoreType.DMA((3, 22)),
            pltpu.SemaphoreType.DMA((2, 4)),
            pltpu.SemaphoreType.DMA((2, 4)),
            pltpu.SemaphoreType.DMA((12,)),
        ],
        compiler_params=pltpu.CompilerParams(
            collective_id=0, has_side_effects=True, vmem_limit_bytes=59 * 1024 * 1024
        ),
    )(tpl_stations.T, det_station, det_time, partner.T, jnp.transpose(waveforms, (1, 0, 2)),
      det_station.reshape(1, DET), det_time.reshape(1, DET), templates.reshape(count, 3 * TB * B),
      jnp.asarray(forward), jnp.asarray(inverse), jnp.asarray(ends))
    return stack, diff


def solution(mesh):
    return jax.shard_map(
        on_device,
        mesh=mesh,
        in_specs=(
            P(("gx", "gy"), None, None),
            P(("gx", "gy"), None, None),
            P(("gx", "gy"), None),
            P(("gx", "gy")),
            P(("gx", "gy")),
            P(("gx", "gy"), None),
        ),
        out_specs=(P(("gx", "gy"), None), P(("gx", "gy"), None, None)),
        check_vma=False,
    )
```
